128 devices in a mesh: gx: 8 (over y_hi, x), yz: 16 (over z, y_lo, core).
Axes of the slice: x: 4, y: 4 (y_hi: 2, y_lo: 2; y = y_hi * 2 + y_lo), z: 4, core: 2. Of those that a mesh axis runs over, the one named last changes fastest.
Arguments:
- decode_rows: bfloat16 [1536, 16384], P('yz', 'gx'), may hold values from -6 to 6
- attended: bfloat16 [1536, 16384], P('yz', 'gx'), may hold values from -6 to 6
- qkv_values: bfloat16 [16384, 18432], P(('gx', 'yz')), may hold values from -6 to 6
- qkv_scales: bfloat16 [128, 144], P(('gx', 'yz')), may hold values from 0.0023345947 to 0.0234375
- out_values: bfloat16 [16384, 16384], P(('gx', 'yz')), may hold values from -6 to 6
- out_scales: bfloat16 [128, 128], P(('gx', 'yz')), may hold values from 0.0023345947 to 0.0234375
Outputs:
- qkv: bfloat16 [1536, 18432], P('gx', 'yz')
- projected: bfloat16 [1536, 16384], P('gx', 'yz')
The draws below stay inside these ranges and needn't reach their ends.
All inputs are finite; a program needn't handle non-finite values.
Results may differ from the reference program's by a relative error of at most 0.005.
Values may be sent and summed in bfloat16 or wider, within the bound.
A program may use at most 128 MiB of HBM per device.

```python
import math
import jax
import jax.numpy as jnp

TILE = 128
ROWS = 1536
D = 16384
QKV = 18432


def block_scale(own_key, shape, split, low, largest):
    gain = 1.0
    for dim, blocks in split:
        draws = jax.random.uniform(jax.random.fold_in(jax.random.fold_in(own_key, 6), dim), (blocks,), jnp.float32, low / len(split), largest / len(split))
        gain = gain * jnp.repeat(jnp.exp(draws), shape[dim] // blocks).reshape((-1,) + (1,) * (len(shape) - 1 - dim))
    return gain


def gaussian(rng, extent, deviation, limit, cuts=(), kind=jnp.bfloat16):
    level = block_scale(rng, extent, cuts, -0.22, 0.18) if cuts else 1.0
    array = jax.random.normal(rng, extent, jnp.float32) * deviation * level
    return jnp.minimum(jnp.maximum(array, -limit), limit).astype(kind)


def setup_inputs(seed: int = 0) -> dict:
    keys = jax.random.split(jax.random.key(seed), 7)
    decode_rows = gaussian(keys[0], (ROWS, D), 1.0, 6.0, ((0, 16), (1, 8)))
    attended = gaussian(keys[1], (ROWS, D), 1.0, 6.0, ((0, 16), (1, 8)))
    qkv_values = gaussian(keys[2], (D, QKV), 1.0, 6.0, ((0, 128),))
    qkv_scales = jnp.clip(jnp.exp(math.log(0.0234375) - 2.306499 * jax.random.uniform(keys[3], (D // TILE, QKV // TILE), jnp.float32) ** block_scale(keys[3], (D // TILE, QKV // TILE), ((0, 128),), -0.2, 0.2)), 0.0023345947, 0.0234375).astype(jnp.bfloat16)
    out_values = gaussian(keys[4], (D, D), 1.0, 6.0, ((0, 128),))
    out_scales = jnp.clip(jnp.exp(math.log(0.0234375) - 2.306499 * jax.random.uniform(keys[5], (D // TILE, D // TILE), jnp.float32) ** block_scale(keys[5], (D // TILE, D // TILE), ((0, 128),), -0.2, 0.2)), 0.0023345947, 0.0234375).astype(jnp.bfloat16)
    return dict(decode_rows=decode_rows, attended=attended, qkv_values=qkv_values, qkv_scales=qkv_scales, out_values=out_values, out_scales=out_scales)


def dequantize(values, scales):
    rows, cols = values.shape
    tiled = values.reshape(rows // TILE, TILE, cols // TILE, TILE).astype(jnp.float32)
    scaled = tiled * scales.astype(jnp.float32)[:, None, :, None]
    return scaled.reshape(rows, cols).astype(jnp.bfloat16)


def reference(decode_rows, attended, qkv_values, qkv_scales, out_values, out_scales):
    qkv_weight = dequantize(qkv_values, qkv_scales)
    out_weight = dequantize(out_values, out_scales)
    qkv = jnp.dot(decode_rows, qkv_weight, preferred_element_type=jnp.float32).astype(jnp.bfloat16)
    projected = jnp.dot(attended, out_weight, preferred_element_type=jnp.float32).astype(jnp.bfloat16)
    return qkv, projected
```

```python
import jax
import jax.numpy as jnp
from jax import lax
from jax.experimental import pallas as pl
from jax.experimental.pallas import tpu as pltpu
from jax.sharding import PartitionSpec as P

MESH = pl.DeviceIdType.MESH
F32 = jnp.float32
BF16 = jnp.bfloat16

QCH, QW = 9, 256
OCH, OW = 4, 512
STEPS = (
    ("q", 0), ("o", 0), ("q", 1), ("q", 2), ("o", 1), ("q", 3), ("q", 4),
    ("o", 2), ("q", 5), ("q", 6), ("o", 3), ("q", 7), ("q", 8),
)


def kernel(
    rows_q, rows_o, val_q, val_o, sc_q, sc_o,
    out_q, out_o,
    in_q, in_o, x_q, x_o, a_q, a_o, snd_q, snd_o, w_q, w_o, p_q, p_o,
    far_q, far_o, rx_q, rx_o, ph_q, ph_o, swap,
    ld, s1s, s1q, s1o, s2s, s2q, s2o, sbs, sbq, sbo,
    wsq, wso, wrq, wro, fsq, fso, frq, fro, rsq, rso, rrq, rro, psq, pso, prq, pro, sws, swr,
):
    g = lax.axis_index("gx")
    w = lax.axis_index("yz")
    x, yh = lax.rem(g, 4), lax.div(g, 4)
    c, yl, z = lax.rem(w, 2), lax.rem(lax.div(w, 2), 2), lax.div(w, 4)
    y = yh * 2 + yl

    def dev(dx=0, dy=0, dz=0, dc=0):
        xx, yy, zz, cc = (lax.rem(x + dx, 4), lax.rem(y + dy, 4), lax.rem(z + dz, 4), lax.rem(c + dc, 2))
        return (lax.div(yy, 2) * 4 + xx, zz * 4 + lax.rem(yy, 2) * 2 + cc)

    mate = (g, z * 4 + (1 - yl) * 2 + c)
    sib = dev(dc=1)

    def remote(src, dst, ssem, rsem, to):
        return pltpu.make_async_remote_copy(
            src_ref=src, dst_ref=dst, send_sem=ssem, recv_sem=rsem, device_id=to, device_id_type=MESH
        )

    def drain(ref, sem):
        pltpu.make_async_copy(ref, ref, sem).wait()

    loads = []
    for half in range(2):
        for zz in range(4):
            loads.append(pltpu.make_async_copy(
                rows_q.at[:, pl.ds(zz * 512 + half * 256, 256)],
                x_q.at[half, :, pl.ds(zz * 256, 256)], ld.at[0]))
    for zz in range(4):
        loads.append(pltpu.make_async_copy(
            rows_o.at[:, pl.ds(zz * 512, 512)], x_o.at[zz], ld.at[1]))
    loads.append(pltpu.make_async_copy(val_q, in_q, ld.at[2]))
    loads.append(pltpu.make_async_copy(val_o, in_o, ld.at[3]))
    for cp in loads:
        cp.start()

    peers = [dev(dy=dy, dz=dz) for dy in range(4) for dz in range(4) if (dy, dz) != (0, 0)]
    peers += [dev(dz=dz, dc=1) for dz in range(4)]
    peers += [dev(dy=dy, dc=1) for dy in range(1, 4)]
    peers += [dev(dx=1), dev(dx=3)]
    barrier = pltpu.get_barrier_semaphore()
    for peer in peers:
        pl.semaphore_signal(barrier, inc=1, device_id=peer, device_id_type=MESH)
    pl.semaphore_wait(barrier, len(peers))

    own_cols = pl.ds(pl.multiple_of(yh * 512, 512), 512)
    drain(x_q, ld.at[0])
    drain(x_o, ld.at[1])
    q1 = remote(x_q.at[1 - yl], a_q.at[z, yl, c], s1s.at[0], s1q.at[0], mate)
    q1.start()
    o1 = []
    for k in (2, 1, 3):
        cp = remote(x_o.at[lax.rem(z + k, 4)], a_o.at[z, yl, c, :, own_cols], s1s.at[k], s1o.at[k], dev(dz=k))
        cp.start()
        o1.append(cp)
    q1l = pltpu.make_async_copy(x_q.at[yl], a_q.at[z, yl, c], s1q.at[1])
    q1l.start()
    o1l = pltpu.make_async_copy(x_o.at[z], a_o.at[z, yl, c, :, own_cols], s1o.at[0])
    o1l.start()

    def weights_q(ch):
        @pl.loop(0, 8)
        def _(d):
            for half in range(2):
                block = lax.div(d, 2) * 4 + half * 2 + lax.rem(d, 2)
                col = pl.multiple_of(block * 1152 + ch * 128, 128)
                s = sc_q[0, block * 9 + ch]
                snd_q[ch, d, :, half * 128:(half + 1) * 128] = (
                    in_q[:, pl.ds(col, 128)].astype(F32) * s).astype(BF16)
        here = pl.ds(pl.multiple_of((z * 2 + c) * 128, 128), 128)
        for k, dc in ((2, 0), (2, 1), (1, 0), (3, 0), (1, 1), (3, 1), (0, 1)):
            slot = lax.rem(z + k, 4) * 2 + lax.rem(c + dc, 2)
            remote(snd_q.at[ch, slot], w_q.at[ch, here], wsq.at[ch], wrq.at[ch], dev(dz=k, dc=dc)).start()
        pltpu.make_async_copy(snd_q.at[ch, z * 2 + c], w_q.at[ch, here], wrq.at[ch]).start()

    def weights_o(ch):
        @pl.loop(0, 8)
        def _(d):
            for zz in range(4):
                block = zz * 4 + lax.rem(d, 4)
                tile = block * 8 + lax.div(d, 4) * 4 + ch
                col = pl.multiple_of(tile * 128, 128)
                s = sc_o[0, tile]
                snd_o[ch, d, :, zz * 128:(zz + 1) * 128] = (
                    in_o[:, pl.ds(col, 128)].astype(F32) * s).astype(BF16)
        here = pl.ds(pl.multiple_of((y * 2 + c) * 128, 128), 128)
        for k, dc in ((2, 0), (2, 1), (1, 0), (3, 0), (1, 1), (3, 1), (0, 1)):
            slot = lax.rem(y + k, 4) * 2 + lax.rem(c + dc, 2)
            remote(snd_o.at[ch, slot], w_o.at[ch, here], wso.at[ch], wro.at[ch], dev(dy=k, dc=dc)).start()
        pltpu.make_async_copy(snd_o.at[ch, y * 2 + c], w_o.at[ch, here], wro.at[ch]).start()

    drain(in_q, ld.at[2])
    weights_q(0)

    q1.wait_recv()
    q1l.wait()
    q2 = []
    mine = a_q.at[z, :, c]
    for k in (2, 1, 3):
        cp = remote(mine, mine, s2s.at[k], s2q.at[k], dev(dz=k))
        cp.start()
        q2.append((k, cp))
    sibs = [remote(mine, mine, sbs.at[0], sbq.at[0], sib)]
    sibs[0].start()
    for cp in o1:
        cp.wait_recv()
    o1l.wait()
    o2 = []
    mine = a_o.at[:, yl, c, :, own_cols]
    for k in (2, 1, 3):
        cp = remote(mine, mine, s2s.at[4 + k], s2o.at[k], dev(dy=k))
        cp.start()
        o2.append((k, cp))
    sibs.append(remote(mine, mine, sbs.at[4], sbo.at[0], sib))
    sibs[-1].start()

    drain(in_o, ld.at[3])
    for p, ch in STEPS[1:]:
        (weights_q if p == "q" else weights_o)(ch)

    for k, cp in q2:
        cp.wait_recv()
        part = a_q.at[lax.rem(z + 4 - k, 4), :, c]
        fw = remote(part, part, sbs.at[k], sbq.at[k], sib)
        fw.start()
        sibs.append(fw)
    for k, cp in o2:
        cp.wait_recv()
        yy = lax.rem(y + 4 - k, 4)
        part = a_o.at[:, lax.rem(yy, 2), c, :, pl.ds(pl.multiple_of(lax.div(yy, 2) * 512, 512), 512)]
        fw = remote(part, part, sbs.at[4 + k], sbo.at[k], sib)
        fw.start()
        sibs.append(fw)
    for cp in sibs:
        cp.wait_recv()

    right, left = dev(dx=1), dev(dx=3)
    xr, xl, xo = lax.rem(x + 1, 4), lax.rem(x + 3, 4), lax.rem(x + 2, 4)
    refs = {
        "q": (a_q, w_q, p_q, far_q, rx_q, wrq, fsq, frq, rsq, rrq),
        "o": (a_o, w_o, p_o, far_o, rx_o, wro, fso, fro, rso, rro),
    }
    width = {"q": QW, "o": OW}

    def compute(p, ch):
        a, wt, part, far, rx, wr, fs, fr, rs, rr = refs[p]
        drain(wt.at[ch], wr.at[ch])

        @pl.loop(0, 4)
        def _(i):
            lhs = a[i].reshape(384, 1024)
            acc = jnp.dot(lhs, wt[ch], preferred_element_type=F32)
            part[ch, lax.div(i, 2), pl.ds(lax.rem(i, 2) * 2, 2)] = acc.astype(BF16).reshape(2, 192, width[p])

        remote(part.at[ch, 1, xo], far.at[ch, 1], fs.at[ch, 1], fr.at[ch, 1], right).start()
        remote(part.at[ch, 0, xo], far.at[ch, 0], fs.at[ch, 0], fr.at[ch, 0], left).start()
        remote(part.at[ch, 0, xr], rx.at[ch, 0], rs.at[ch, 0], rr.at[ch, 0], right).start()
        remote(part.at[ch, 1, xl], rx.at[ch, 1], rs.at[ch, 1], rr.at[ch, 1], left).start()

    def relay(p, ch):
        a, wt, part, far, rx, wr, fs, fr, rs, rr = refs[p]
        drain(far.at[ch, 1], fr.at[ch, 1])
        part[ch, 1, xr] = (part[ch, 1, xr].astype(F32) + far[ch, 1].astype(F32)).astype(BF16)
        remote(part.at[ch, 1, xr], rx.at[ch, 2], rs.at[ch, 2], rr.at[ch, 2], right).start()
        drain(far.at[ch, 0], fr.at[ch, 0])
        part[ch, 0, xl] = (part[ch, 0, xl].astype(F32) + far[ch, 0].astype(F32)).astype(BF16)
        remote(part.at[ch, 0, xl], rx.at[ch, 3], rs.at[ch, 3], rr.at[ch, 3], left).start()

    def collect(p, ch):
        a, wt, part, far, rx, wr, fs, fr, rs, rr = refs[p]
        for h, (i, j) in enumerate(((0, 3), (1, 2))):
            drain(rx.at[ch, i], rr.at[ch, i])
            drain(rx.at[ch, j], rr.at[ch, j])
            part[ch, h, x] = (part[ch, h, x].astype(F32) + rx[ch, i].astype(F32) + rx[ch, j].astype(F32)).astype(BF16)
        if p == "q":
            for k in (2, 1, 3):
                yy = lax.rem(y + k, 4)
                cols = pl.ds(pl.multiple_of(lax.rem(yy, 2) * 128, 128), 128)
                remote(part.at[ch, lax.div(yy, 2), x, :, cols], ph_q.at[ch, k - 1],
                       psq.at[ch, k - 1], prq.at[ch, k - 1], dev(dy=k)).start()
        else:
            for k in (2, 1, 3):
                cols = pl.ds(pl.multiple_of(lax.rem(z + k, 4) * 128, 128), 128)
                remote(part.at[ch, :, x, :, cols], ph_o.at[ch, k - 1],
                       pso.at[ch, k - 1], pro.at[ch, k - 1], dev(dz=k)).start()

    def finish(p, ch):
        if p == "q":
            cols = pl.ds(pl.multiple_of(yl * 128, 128), 128)
            total = p_q[ch, yh, x, :, cols].astype(F32)
            for k in range(3):
                drain(ph_q.at[ch, k], prq.at[ch, k])
                total += ph_q[ch, k].astype(F32)
            out_q[:, ch * 128:(ch + 1) * 128] = total.astype(BF16)
        else:
            cols = pl.ds(pl.multiple_of(z * 128, 128), 128)
            for k in range(3):
                drain(ph_o.at[ch, k], pro.at[ch, k])
            give, keep = 1 - yh, yh
            for h in (give, keep):
                total = p_o[ch, h, x, :, cols].astype(F32)
                for k in range(3):
                    total += ph_o[ch, k, h].astype(F32)
                if h is give:
                    swap[0, ch] = total.astype(BF16)
                    remote(swap.at[0, ch], swap.at[1, ch], sws.at[ch], swr.at[ch], dev(dy=2)).start()
                else:
                    out_o[:, pl.ds(pl.multiple_of(yh * 512 + ch * 128, 128), 128)] = total.astype(BF16)

    def settle(ch):
        drain(swap.at[1, ch], swr.at[ch])
        out_o[:, pl.ds(pl.multiple_of((1 - yh) * 512 + ch * 128, 128), 128)] = swap[1, ch]

    n = len(STEPS)
    for i in range(n + 4):
        if i < n:
            compute(*STEPS[i])
        if 1 <= i < n + 1:
            relay(*STEPS[i - 1])
        if 2 <= i < n + 2:
            collect(*STEPS[i - 2])
        if 4 <= i < n + 4:
            finish(*STEPS[i - 4])
    for ch in range(OCH):
        settle(ch)

    q1.wait_send()
    for cp in o1 + [cp for _, cp in q2 + o2] + sibs:
        cp.wait_send()
    for ch in range(QCH):
        drain(snd_q.at[ch, pl.ds(0, 7)], wsq.at[ch])
    for ch in range(OCH):
        drain(snd_o.at[ch, pl.ds(0, 7)], wso.at[ch])
        drain(swap.at[0, ch], sws.at[ch])
    for p, ch in STEPS:
        a, wt, part, far, rx, wr, fs, fr, rs, rr = refs[p]
        for i in range(2):
            drain(far.at[ch, i], fs.at[ch, i])
        for i in range(4):
            drain(rx.at[ch, i], rs.at[ch, i])
        ph, ps = (ph_q, psq) if p == "q" else (ph_o, pso)
        for k in range(3):
            drain(ph.at[ch, k], ps.at[ch, k])


def local(decode_rows, attended, qkv_values, qkv_scales, out_values, out_scales):
    dma = pltpu.SemaphoreType.DMA
    vmem = pltpu.VMEM
    return pl.pallas_call(
        kernel,
        out_shape=(
            jax.ShapeDtypeStruct((192, 1152), BF16),
            jax.ShapeDtypeStruct((192, 1024), BF16),
        ),
        in_specs=[pl.BlockSpec(memory_space=pl.ANY)] * 4 + [pl.BlockSpec(memory_space=pltpu.SMEM)] * 2,
        out_specs=(pl.BlockSpec(memory_space=vmem), pl.BlockSpec(memory_space=vmem)),
        scratch_shapes=[
            vmem((128, 18432), BF16), vmem((128, 16384), BF16),
            vmem((2, 96, 1024), BF16), vmem((4, 96, 512), BF16),
            vmem((4, 2, 2, 96, 1024), BF16), vmem((4, 2, 2, 96, 1024), BF16),
            vmem((QCH, 8, 128, QW), BF16), vmem((OCH, 8, 128, OW), BF16),
            vmem((QCH, 1024, QW), BF16), vmem((OCH, 1024, OW), BF16),
            vmem((QCH, 2, 4, 192, QW), BF16), vmem((OCH, 2, 4, 192, OW), BF16),
            vmem((QCH, 2, 192, QW), BF16), vmem((OCH, 2, 192, OW), BF16),
            vmem((QCH, 4, 192, QW), BF16), vmem((OCH, 4, 192, OW), BF16),
            vmem((QCH, 3, 192, 128), BF16), vmem((OCH, 3, 2, 192, 128), BF16),
            vmem((2, OCH, 192, 128), BF16),
            dma((4,)), dma((4,)), dma((2,)), dma((4,)), dma((8,)), dma((4,)), dma((4,)),
            dma((8,)), dma((4,)), dma((4,)),
            dma((QCH,)), dma((OCH,)), dma((QCH,)), dma((OCH,)),
            dma((QCH, 2)), dma((OCH, 2)), dma((QCH, 2)), dma((OCH, 2)),
            dma((QCH, 4)), dma((OCH, 4)), dma((QCH, 4)), dma((OCH, 4)),
            dma((QCH, 3)), dma((OCH, 3)), dma((QCH, 3)), dma((OCH, 3)),
            dma((OCH,)), dma((OCH,)),
        ],
        compiler_params=pltpu.CompilerParams(
            collective_id=0, has_side_effects=True, vmem_limit_bytes=63 * 2**20
        ),
        cost_estimate=pl.CostEstimate(flops=13_690_000_000, bytes_accessed=20_000_000, transcendentals=0),
        name="project",
    )(
        decode_rows, attended, qkv_values, out_values,
        qkv_scales.astype(F32), out_scales.astype(F32),
    )


def solution(mesh):
    in_specs = (
        P("yz", "gx"),
        P("yz", "gx"),
        P(("gx", "yz"), None),
        P(("gx", "yz"), None),
        P(("gx", "yz"), None),
        P(("gx", "yz"), None),
    )
    out_specs = (P("gx", "yz"), P("gx", "yz"))
    return jax.shard_map(local, mesh=mesh, in_specs=in_specs, out_specs=out_specs, check_vma=False)
```

```python
import jax
import jax.numpy as jnp
from jax import lax
from jax.experimental import pallas as pl
from jax.experimental.pallas import tpu as pltpu
from jax.sharding import PartitionSpec as P

MESH = pl.DeviceIdType.MESH
F32 = jnp.float32
BF16 = jnp.bfloat16

QCH, QW = 9, 256
OCH, OW = 4, 512
SWAPPED = (("o", 3), ("q", 4), ("q", 5), ("q", 6), ("q", 7), ("q", 8),)
CHUNKS = tuple(("q", i) for i in range(QCH)) + tuple(("o", i) for i in range(OCH))
PLACE = {}
for _p in "qo":
    for _kind in (False, True):
        for _i, _t in enumerate(t for t in CHUNKS if t[0] == _p and (t in SWAPPED) == _kind):
            PLACE[_t] = _i
NQS, NOS = (sum(t[0] == p for t in SWAPPED) for p in "qo")
OPS = (
    ("q1",), ("o1",), ("w", "q", 0), ("q2",), ("o2",), ("w", "o", 0), ("w", "q", 1), ("w", "q", 2),
    ("w", "o", 1), ("w", "q", 3), ("w", "q", 4), ("w", "o", 2), ("w", "q", 5), ("w", "q", 6), ("w", "o", 3),
    ("w", "q", 7), ("w", "q", 8), ("F", "q", 2), ("F", "o", 1), ("F", "o", 2), ("F", "o", 3), ("F", "q", 1),
    ("F", "q", 3), ("c", "q", 0), ("c", "q", 1), ("c", "o", 0), ("r", "q", 0), ("c", "q", 2), ("r", "q", 1),
    ("c", "q", 3), ("r", "o", 0), ("c", "o", 1), ("c", "q", 4), ("k", "q", 0), ("r", "q", 2), ("c", "o", 2),
    ("k", "q", 1), ("c", "q", 5), ("r", "q", 3), ("c", "q", 6), ("k", "o", 0), ("c", "o", 3), ("r", "q", 4),
    ("c", "q", 7), ("r", "o", 1), ("f", "q", 0), ("c", "q", 8), ("f", "q", 1), ("k", "q", 2), ("r", "q", 5),
    ("f", "o", 0), ("r", "o", 2), ("r", "q", 6), ("r", "o", 3), ("k", "q", 4), ("k", "q", 3), ("r", "q", 7),
    ("k", "o", 3), ("r", "q", 8), ("k", "o", 1), ("k", "o", 2), ("f", "q", 2), ("f", "q", 4), ("k", "q", 5),
    ("f", "o", 1), ("k", "q", 6), ("f", "o", 3), ("f", "q", 3), ("f", "q", 5), ("f", "o", 2), ("k", "q", 7),
    ("f", "q", 6), ("k", "q", 8), ("f", "q", 7), ("f", "q", 8),
)


def kernel(
    rows_q, rows_o, val_q, val_o, scale_q, scale_o,
    out_q, out_o,
    in_q, in_o, x_q, x_o, a_q, a_o, snd_q, snd_o, w_q, w_o, p_q, p_o,
    far_q, far_o, far_qs, far_os, rx_q, rx_o, rx_qs, rx_os, ph_q, ph_o, swap, scf_q, scf_o, sc_q, sc_o,
    ld, s1s, s1q, s1o, s2s, s2q, s2o, sbs, sbq, sbo,
    wsq, wso, wrq, wro, fsq, fso, frq, fro, rsq, rso, rrq, rro, psq, pso, prq, pro, sws, swr,
):
    g = lax.axis_index("gx")
    w = lax.axis_index("yz")
    x, yh = lax.rem(g, 4), lax.div(g, 4)
    c, yl, z = lax.rem(w, 2), lax.rem(lax.div(w, 2), 2), lax.div(w, 4)
    y = yh * 2 + yl

    def dev(dx=0, dy=0, dz=0, dc=0):
        xx, yy, zz, cc = (lax.rem(x + dx, 4), lax.rem(y + dy, 4), lax.rem(z + dz, 4), lax.rem(c + dc, 2))
        return (lax.div(yy, 2) * 4 + xx, zz * 4 + lax.rem(yy, 2) * 2 + cc)

    mate = (g, z * 4 + (1 - yl) * 2 + c)
    sib = dev(dc=1)

    def remote(src, dst, ssem, rsem, to):
        return pltpu.make_async_remote_copy(
            src_ref=src, dst_ref=dst, send_sem=ssem, recv_sem=rsem, device_id=to, device_id_type=MESH
        )

    def drain(ref, sem):
        pltpu.make_async_copy(ref, ref, sem).wait()

    loads = []
    for half in range(2):
        for zz in range(4):
            loads.append(pltpu.make_async_copy(
                rows_q.at[:, pl.ds(zz * 512 + half * 256, 256)],
                x_q.at[half, :, pl.ds(zz * 256, 256)], ld.at[0]))
    for zz in range(4):
        loads.append(pltpu.make_async_copy(
            rows_o.at[:, pl.ds(zz * 512, 512)], x_o.at[zz], ld.at[1]))
    loads.append(pltpu.make_async_copy(val_q, in_q, ld.at[2]))
    loads.append(pltpu.make_async_copy(val_o, in_o, ld.at[3]))
    for cp in loads:
        cp.start()

    scf_q[...] = scale_q[...].astype(F32)
    scf_o[...] = scale_o[...].astype(F32)
    for src, dst, sem in ((scf_q, sc_q, ld.at[4]), (scf_o, sc_o, ld.at[5])):
        cp = pltpu.make_async_copy(src, dst, sem)
        cp.start()
        loads.append(cp)

    peers = [dev(dy=dy, dz=dz) for dy in range(4) for dz in range(4) if (dy, dz) != (0, 0)]
    peers += [dev(dz=dz, dc=1) for dz in range(4)]
    peers += [dev(dy=dy, dc=1) for dy in range(1, 4)]
    peers += [dev(dx=1), dev(dx=2), dev(dx=3)]
    barrier = pltpu.get_barrier_semaphore()
    for peer in peers:
        pl.semaphore_signal(barrier, inc=1, device_id=peer, device_id_type=MESH)
    pl.semaphore_wait(barrier, len(peers))

    own_cols = pl.ds(pl.multiple_of(yh * 512, 512), 512)
    pending = []
    stage = {}

    def first_q():
        drain(x_q, ld.at[0])
        cp = remote(x_q.at[1 - yl], a_q.at[z, yl, c], s1s.at[0], s1q.at[0], mate)
        cp.start()
        here = pltpu.make_async_copy(x_q.at[yl], a_q.at[z, yl, c], s1q.at[1])
        here.start()
        stage["q"] = [cp], here

    def first_o():
        drain(x_o, ld.at[1])
        cps = []
        for k in (2, 1, 3):
            cp = remote(x_o.at[lax.rem(z + k, 4)], a_o.at[z, yl, c, :, own_cols], s1s.at[k], s1o.at[k], dev(dz=k))
            cp.start()
            cps.append(cp)
        here = pltpu.make_async_copy(x_o.at[z], a_o.at[z, yl, c, :, own_cols], s1o.at[0])
        here.start()
        stage["o"] = cps, here

    def second(p):
        cps, here = stage[p]
        for cp in cps:
            cp.wait_recv()
        here.wait()
        pending.extend(cps)
        if p == "q":
            mine, ss, rs, bs, br = a_q.at[z, :, c], 0, s2q, 0, sbq
        else:
            mine, ss, rs, bs, br = a_o.at[:, yl, c, :, own_cols], 4, s2o, 4, sbo
        for k in (2, 1, 3):
            cp = remote(mine, mine, s2s.at[ss + k], rs.at[k], dev(dz=k) if p == "q" else dev(dy=k))
            cp.start()
            stage[p, k] = cp
            pending.append(cp)
        cp = remote(mine, mine, sbs.at[bs], br.at[0], sib)
        cp.start()
        stage[p, "sib"] = [cp]

    def forward(p, k):
        stage[p, k].wait_recv()
        if p == "q":
            part = a_q.at[lax.rem(z + 4 - k, 4), :, c]
            cp = remote(part, part, sbs.at[k], sbq.at[k], sib)
        else:
            yy = lax.rem(y + 4 - k, 4)
            part = a_o.at[:, lax.rem(yy, 2), c, :, pl.ds(pl.multiple_of(lax.div(yy, 2) * 512, 512), 512)]
            cp = remote(part, part, sbs.at[4 + k], sbo.at[k], sib)
        cp.start()
        stage[p, "sib"].append(cp)

    def rows_ready(p):
        for cp in stage.pop((p, "sib"), []):
            cp.wait_recv()
            pending.append(cp)

    def weights_q(ch):
        @pl.loop(0, 8)
        def _(d):
            for half in range(2):
                block = lax.div(d, 2) * 4 + half * 2 + lax.rem(d, 2)
                col = pl.multiple_of(block * 1152 + ch * 128, 128)
                s = sc_q[0, block * 9 + ch]
                snd_q[ch, d, :, half * 128:(half + 1) * 128] = (
                    in_q[:, pl.ds(col, 128)].astype(F32) * s).astype(BF16)
        here = pl.ds(pl.multiple_of((z * 2 + c) * 128, 128), 128)
        for k, dc in ((2, 0), (2, 1), (1, 0), (3, 0), (1, 1), (3, 1), (0, 1)):
            slot = lax.rem(z + k, 4) * 2 + lax.rem(c + dc, 2)
            remote(snd_q.at[ch, slot], w_q.at[ch, here], wsq.at[ch], wrq.at[ch], dev(dz=k, dc=dc)).start()
        pltpu.make_async_copy(snd_q.at[ch, z * 2 + c], w_q.at[ch, here], wrq.at[ch]).start()

    def weights_o(ch):
        @pl.loop(0, 8)
        def _(d):
            for zz in range(4):
                block = zz * 4 + lax.rem(d, 4)
                tile = block * 8 + lax.div(d, 4) * 4 + ch
                col = pl.multiple_of(tile * 128, 128)
                s = sc_o[0, tile]
                snd_o[ch, d, :, zz * 128:(zz + 1) * 128] = (
                    in_o[:, pl.ds(col, 128)].astype(F32) * s).astype(BF16)
        here = pl.ds(pl.multiple_of((y * 2 + c) * 128, 128), 128)
        for k, dc in ((2, 0), (2, 1), (1, 0), (3, 0), (1, 1), (3, 1), (0, 1)):
            slot = lax.rem(y + k, 4) * 2 + lax.rem(c + dc, 2)
            remote(snd_o.at[ch, slot], w_o.at[ch, here], wso.at[ch], wro.at[ch], dev(dy=k, dc=dc)).start()
        pltpu.make_async_copy(snd_o.at[ch, y * 2 + c], w_o.at[ch, here], wro.at[ch]).start()

    loaded = set()

    def weights(p, ch):
        if p not in loaded:
            loaded.add(p)
            i = "qo".index(p)
            drain((in_q, in_o)[i], ld.at[2 + i])
            loads[-2 + i].wait()
        (weights_q if p == "q" else weights_o)(ch)

    class Chunk:
        def __init__(self, p, ch):
            swapped = (p, ch) in SWAPPED
            at = PLACE[p, ch]
            self.p, self.ch, self.swapped = p, ch, swapped
            self.part = p_q if p == "q" else p_o
            if p == "q":
                self.far, self.rx = (far_qs, rx_qs) if swapped else (far_q, rx_q)
                self.far_sems, self.rx_sems = (fsq, frq), (rsq, rrq)
            else:
                self.far, self.rx = (far_os, rx_os) if swapped else (far_o, rx_o)
                self.far_sems, self.rx_sems = (fso, fro), (rso, rro)
            self.far, self.rx = self.far.at[at], self.rx.at[at]
            if not swapped:
                self.me, self.right, self.left = x, dev(dx=1), dev(dx=3)
            elif p == "q":
                self.me, self.right, self.left = y, dev(dy=1), dev(dy=3)
            else:
                self.me, self.right, self.left = z, dev(dz=1), dev(dz=3)

        def block(self, ahead, half):
            to = lax.rem(self.me + ahead, 4)
            if not self.swapped:
                return self.part.at[self.ch, half, to]
            if self.p == "q":
                cols = pl.ds(pl.multiple_of(lax.rem(to, 2) * 128, 128), 128)
                return self.part.at[self.ch, lax.div(to, 2), pl.ds(2 * half, 2), :, cols]
            cols = pl.ds(pl.multiple_of(to * 128, 128), 128)
            return self.part.at[self.ch, half, :, :, cols]

        def send_far(self, src, half, to):
            ss, rs = self.far_sems
            remote(src, self.far.at[half], ss.at[self.ch, half], rs.at[self.ch, half], to).start()

        def send_sum(self, src, slot, to):
            ss, rs = self.rx_sems
            remote(src, self.rx.at[slot], ss.at[self.ch, slot], rs.at[self.ch, slot], to).start()

    def compute(p, ch):
        t = Chunk(p, ch)
        a, wt, wr, wide = (a_q, w_q, wrq, QW) if p == "q" else (a_o, w_o, wro, OW)
        rows_ready(p)
        drain(wt.at[ch], wr.at[ch])

        @pl.loop(0, 4)
        def _(i):
            lhs = a[i].reshape(384, 1024)
            acc = jnp.dot(lhs, wt[ch], preferred_element_type=F32)
            t.part[ch, lax.div(i, 2), pl.ds(lax.rem(i, 2) * 2, 2)] = acc.astype(BF16).reshape(2, 192, wide)

        t.send_far(t.block(2, 1), 1, t.right)
        t.send_far(t.block(2, 0), 0, t.left)
        t.send_sum(t.block(1, 0), 0, t.right)
        t.send_sum(t.block(3, 1), 1, t.left)

    def relay(p, ch):
        t = Chunk(p, ch)
        for half, ahead, slot, to in ((1, 1, 2, t.right), (0, 3, 3, t.left)):
            drain(t.far.at[half], t.far_sems[1].at[ch, half])
            own = t.block(ahead, half)
            own[...] = (own[...].astype(F32) + t.far[half].astype(F32)).astype(BF16)
            t.send_sum(own, slot, to)

    def collect(p, ch):
        t = Chunk(p, ch)
        for half, (i, j) in enumerate(((0, 3), (1, 2))):
            drain(t.rx.at[i], t.rx_sems[1].at[ch, i])
            drain(t.rx.at[j], t.rx_sems[1].at[ch, j])
            own = t.block(0, half)
            own[...] = (own[...].astype(F32) + t.rx[i].astype(F32) + t.rx[j].astype(F32)).astype(BF16)
        for k in (2, 1, 3):
            xx, yy, zz = lax.rem(x + k, 4), lax.rem(y + k, 4), lax.rem(z + k, 4)
            if p == "q":
                hh, ll = (yh, yl) if t.swapped else (lax.div(yy, 2), lax.rem(yy, 2))
                src = p_q.at[ch, hh, xx if t.swapped else x, :, pl.ds(pl.multiple_of(ll * 128, 128), 128)]
                to = dev(dx=k) if t.swapped else dev(dy=k)
                remote(src, ph_q.at[ch, k - 1], psq.at[ch, k - 1], prq.at[ch, k - 1], to).start()
            else:
                cols = pl.ds(pl.multiple_of((z if t.swapped else zz) * 128, 128), 128)
                src = p_o.at[ch, :, xx if t.swapped else x, :, cols]
                to = dev(dx=k) if t.swapped else dev(dz=k)
                remote(src, ph_o.at[ch, k - 1], pso.at[ch, k - 1], pro.at[ch, k - 1], to).start()

    def finish(p, ch):
        if p == "q":
            cols = pl.ds(pl.multiple_of(yl * 128, 128), 128)
            total = p_q[ch, yh, x, :, cols].astype(F32)
            for k in range(3):
                drain(ph_q.at[ch, k], prq.at[ch, k])
                total += ph_q[ch, k].astype(F32)
            out_q[:, ch * 128:(ch + 1) * 128] = total.astype(BF16)
        else:
            cols = pl.ds(pl.multiple_of(z * 128, 128), 128)
            for k in range(3):
                drain(ph_o.at[ch, k], pro.at[ch, k])
            give, keep = 1 - yh, yh
            for h in (give, keep):
                total = p_o[ch, h, x, :, cols].astype(F32)
                for k in range(3):
                    total += ph_o[ch, k, h].astype(F32)
                if h is give:
                    swap[0, ch] = total.astype(BF16)
                    remote(swap.at[0, ch], swap.at[1, ch], sws.at[ch], swr.at[ch], dev(dy=2)).start()
                else:
                    out_o[:, pl.ds(pl.multiple_of(yh * 512 + ch * 128, 128), 128)] = total.astype(BF16)

    def settle(ch):
        drain(swap.at[1, ch], swr.at[ch])
        out_o[:, pl.ds(pl.multiple_of((1 - yh) * 512 + ch * 128, 128), 128)] = swap[1, ch]

    todo = {
        "q1": first_q, "o1": first_o, "q2": lambda: second("q"), "o2": lambda: second("o"),
        "F": forward, "w": weights, "c": compute, "r": relay, "k": collect, "f": finish,
    }
    for op in OPS:
        todo[op[0]](*op[1:])
    for ch in range(OCH):
        settle(ch)

    for cp in pending:
        cp.wait_send()
    for ch in range(QCH):
        drain(snd_q.at[ch, pl.ds(0, 7)], wsq.at[ch])
    for ch in range(OCH):
        drain(snd_o.at[ch, pl.ds(0, 7)], wso.at[ch])
        drain(swap.at[0, ch], sws.at[ch])
    for p, ch in CHUNKS:
        t = Chunk(p, ch)
        for i in range(2):
            drain(t.far.at[i], t.far_sems[0].at[ch, i])
        for i in range(4):
            drain(t.rx.at[i], t.rx_sems[0].at[ch, i])
        ph, ps = (ph_q, psq) if p == "q" else (ph_o, pso)
        for k in range(3):
            drain(ph.at[ch, k], ps.at[ch, k])


def place_kernel(a, b, out_a, out_b):
    out_a[...] = a[...]
    out_b[...] = b[...]


def local(decode_rows, attended, qkv_values, qkv_scales, out_values, out_scales):
    dma = pltpu.SemaphoreType.DMA
    vmem = pltpu.VMEM
    sums = pl.pallas_call(
        kernel,
        out_shape=(
            jax.ShapeDtypeStruct((192, 1152), BF16),
            jax.ShapeDtypeStruct((192, 1024), BF16),
        ),
        in_specs=[pl.BlockSpec(memory_space=pl.ANY)] * 4 + [pl.BlockSpec(memory_space=vmem)] * 2,
        out_specs=(pl.BlockSpec(memory_space=vmem), pl.BlockSpec(memory_space=vmem)),
        scratch_shapes=[
            vmem((128, 18432), BF16), vmem((128, 16384), BF16),
            vmem((2, 96, 1024), BF16), vmem((4, 96, 512), BF16),
            vmem((4, 2, 2, 96, 1024), BF16), vmem((4, 2, 2, 96, 1024), BF16),
            vmem((QCH, 8, 128, QW), BF16), vmem((OCH, 8, 128, OW), BF16),
            vmem((QCH, 1024, QW), BF16), vmem((OCH, 1024, OW), BF16),
            vmem((QCH, 2, 4, 192, QW), BF16), vmem((OCH, 2, 4, 192, OW), BF16),
            vmem((QCH - NQS, 2, 192, QW), BF16), vmem((OCH - NOS, 2, 192, OW), BF16),
            vmem((NQS, 2, 2, 192, 128), BF16), vmem((NOS, 2, 4, 192, 128), BF16),
            vmem((QCH - NQS, 4, 192, QW), BF16), vmem((OCH - NOS, 4, 192, OW), BF16),
            vmem((NQS, 4, 2, 192, 128), BF16), vmem((NOS, 4, 4, 192, 128), BF16),
            vmem((QCH, 3, 192, 128), BF16), vmem((OCH, 3, 2, 192, 128), BF16),
            vmem((2, OCH, 192, 128), BF16),
            vmem((1, 144), F32), vmem((1, 128), F32), pltpu.SMEM((1, 144), F32), pltpu.SMEM((1, 128), F32),
            dma((6,)), dma((4,)), dma((2,)), dma((4,)), dma((8,)), dma((4,)), dma((4,)),
            dma((8,)), dma((4,)), dma((4,)),
            dma((QCH,)), dma((OCH,)), dma((QCH,)), dma((OCH,)),
            dma((QCH, 2)), dma((OCH, 2)), dma((QCH, 2)), dma((OCH, 2)),
            dma((QCH, 4)), dma((OCH, 4)), dma((QCH, 4)), dma((OCH, 4)),
            dma((QCH, 3)), dma((OCH, 3)), dma((QCH, 3)), dma((OCH, 3)),
            dma((OCH,)), dma((OCH,)),
        ],
        compiler_params=pltpu.CompilerParams(
            collective_id=0, has_side_effects=True, vmem_limit_bytes=63 * 2**20
        ),
        cost_estimate=pl.CostEstimate(flops=13_690_000_000, bytes_accessed=20_000_000, transcendentals=0),
        name="project",
    )(
        decode_rows, attended, qkv_values, out_values,
        qkv_scales, out_scales,
    )
    return pl.pallas_call(
        place_kernel,
        out_shape=tuple(jax.ShapeDtypeStruct(s.shape, BF16) for s in sums),
        in_specs=[pl.BlockSpec(memory_space=vmem)] * 2,
        out_specs=tuple([pl.BlockSpec(memory_space=vmem)] * 2),
        compiler_params=pltpu.CompilerParams(vmem_limit_bytes=4 * 2**20),
        name="place",
    )(*sums)


def solution(mesh):
    in_specs = (
        P("yz", "gx"),
        P("yz", "gx"),
        P(("gx", "yz"), None),
        P(("gx", "yz"), None),
        P(("gx", "yz"), None),
        P(("gx", "yz"), None),
    )
    out_specs = (P("gx", "yz"), P("gx", "yz"))
    return jax.shard_map(local, mesh=mesh, in_specs=in_specs, out_specs=out_specs, check_vma=False)
```

```python
import jax
import jax.numpy as jnp
from jax import lax
from jax.experimental import pallas as pl
from jax.experimental.pallas import tpu as pltpu
from jax.sharding import PartitionSpec as P

MESH = pl.DeviceIdType.MESH
F32 = jnp.float32
BF16 = jnp.bfloat16

QCH, QW = 9, 256
OCH, OW = 4, 512
SWAPPED = (("o", 1), ("q", 0), ("q", 1), ("q", 2), ("q", 4), ("q", 6),)
CHUNKS = tuple(("q", i) for i in range(QCH)) + tuple(("o", i) for i in range(OCH))
PLACE = {}
for _p in "qo":
    for _kind in (False, True):
        for _i, _t in enumerate(t for t in CHUNKS if t[0] == _p and (t in SWAPPED) == _kind):
            PLACE[_t] = _i
NQS, NOS = (sum(t[0] == p for t in SWAPPED) for p in "qo")
OPS = (
    ("o1",), ("q1",), ("w", "o", 0), ("o2",), ("q2",), ("F", "q", 0, 1), ("F", "q", 0, 3), ("w", "q", 3),
    ("w", "o", 3), ("F", "q", 1, 1), ("F", "q", 1, 3), ("w", "q", 7), ("w", "q", 8), ("F", "q", 0, 2),
    ("w", "q", 5), ("w", "q", 4), ("w", "q", 1), ("F", "q", 1, 2), ("F", "o", 0, 1), ("F", "o", 0, 3),
    ("c", "q", 3), ("c", "q", 7), ("w", "o", 2), ("w", "o", 1), ("r", "q", 3), ("c", "q", 8), ("r", "q", 7),
    ("F", "o", 0, 2), ("k", "q", 3), ("w", "q", 0), ("c", "q", 5), ("r", "q", 8), ("c", "o", 0),
    ("c", "o", 3), ("k", "q", 7), ("r", "q", 5), ("c", "q", 4), ("w", "q", 2), ("w", "q", 6), ("k", "q", 8),
    ("c", "q", 1), ("c", "o", 2), ("r", "o", 0), ("c", "q", 0), ("c", "o", 1), ("f", "q", 3), ("c", "q", 2),
    ("r", "o", 3), ("f", "q", 7), ("r", "q", 4), ("c", "q", 6), ("k", "q", 5), ("f", "q", 8), ("r", "q", 1),
    ("r", "o", 1), ("r", "o", 2), ("r", "q", 0), ("r", "q", 2), ("k", "o", 1), ("k", "o", 0), ("k", "q", 4),
    ("k", "o", 3), ("r", "q", 6), ("k", "o", 2), ("f", "o", 0), ("f", "q", 5), ("k", "q", 1), ("f", "o", 1),
    ("f", "o", 3), ("k", "q", 0), ("f", "q", 4), ("k", "q", 2), ("f", "q", 1), ("f", "o", 2), ("k", "q", 6),
    ("f", "q", 0), ("f", "q", 2), ("f", "q", 6),
)


def kernel(
    rows_q, rows_o, val_q, val_o, scale_q, scale_o,
    out_q, out_o,
    in_q, in_o, x_q, x_o, a_q, a_o, snd_q, snd_o, w_q, w_o, p_q, p_o,
    far_q, far_o, far_qs, far_os, rx_q, rx_o, rx_qs, rx_os, ph_q, ph_o, swap, scf_q, scf_o, sc_q, sc_o,
    ld, s1s, s1q, s1o, s2s, s2r,
    wsq, wso, wrq, wro, fsq, fso, frq, fro, rsq, rso, rrq, rro, psq, pso, prq, pro, sws, swr,
):
    g = lax.axis_index("gx")
    w = lax.axis_index("yz")
    x, yh = lax.rem(g, 4), lax.div(g, 4)
    c, yl, z = lax.rem(w, 2), lax.rem(lax.div(w, 2), 2), lax.div(w, 4)
    y = yh * 2 + yl

    def dev(dx=0, dy=0, dz=0, dc=0):
        xx, yy, zz, cc = (lax.rem(x + dx, 4), lax.rem(y + dy, 4), lax.rem(z + dz, 4), lax.rem(c + dc, 2))
        return (lax.div(yy, 2) * 4 + xx, zz * 4 + lax.rem(yy, 2) * 2 + cc)

    mate = (g, z * 4 + (1 - yl) * 2 + c)
    sib = dev(dc=1)

    def remote(src, dst, ssem, rsem, to):
        return pltpu.make_async_remote_copy(
            src_ref=src, dst_ref=dst, send_sem=ssem, recv_sem=rsem, device_id=to, device_id_type=MESH
        )

    def drain(ref, sem):
        pltpu.make_async_copy(ref, ref, sem).wait()

    loads = []
    for half in range(2):
        for zz in range(4):
            loads.append(pltpu.make_async_copy(
                rows_q.at[:, pl.ds(zz * 512 + half * 256, 256)],
                x_q.at[half, :, pl.ds(zz * 256, 256)], ld.at[0]))
    for zz in range(4):
        loads.append(pltpu.make_async_copy(
            rows_o.at[:, pl.ds(zz * 512, 512)], x_o.at[zz], ld.at[1]))
    loads.append(pltpu.make_async_copy(val_q, in_q, ld.at[2]))
    loads.append(pltpu.make_async_copy(val_o, in_o, ld.at[3]))
    for cp in loads:
        cp.start()

    scf_q[...] = scale_q[...].astype(F32)
    scf_o[...] = scale_o[...].astype(F32)
    for src, dst, sem in ((scf_q, sc_q, ld.at[4]), (scf_o, sc_o, ld.at[5])):
        cp = pltpu.make_async_copy(src, dst, sem)
        cp.start()
        loads.append(cp)

    peers = [dev(dy=dy, dz=dz) for dy in range(4) for dz in range(4) if (dy, dz) != (0, 0)]
    peers += [dev(dz=dz, dc=1) for dz in range(4)]
    peers += [dev(dy=dy, dc=1) for dy in range(1, 4)]
    peers += [dev(dx=1), dev(dx=2), dev(dx=3)]
    barrier = pltpu.get_barrier_semaphore()
    for peer in peers:
        pl.semaphore_signal(barrier, inc=1, device_id=peer, device_id_type=MESH)
    pl.semaphore_wait(barrier, len(peers))

    own_cols = pl.ds(pl.multiple_of(yh * 512, 512), 512)
    pending = []
    stage = {}

    def first_q():
        drain(x_q, ld.at[0])
        cp = remote(x_q.at[1 - yl], a_q.at[z, yl, c], s1s.at[0], s1q.at[0], mate)
        cp.start()
        here = pltpu.make_async_copy(x_q.at[yl], a_q.at[z, yl, c], s1q.at[1])
        here.start()
        stage["q"] = [cp], here
        stream("q", 0, x_q.at[yl])

    def first_o():
        drain(x_o, ld.at[1])
        cps = []
        for k in (2, 1, 3):
            cp = remote(x_o.at[lax.rem(z + k, 4)], a_o.at[z, yl, c, :, own_cols], s1s.at[k], s1o.at[k], dev(dz=k))
            cp.start()
            cps.append(cp)
        here = pltpu.make_async_copy(x_o.at[z], a_o.at[z, yl, c, :, own_cols], s1o.at[0])
        here.start()
        stage["o"] = cps, here

    def piece(p, sid, back):
        if p == "q":
            return a_q.at[lax.rem(z + 4 - back, 4), yl if sid == 0 else 1 - yl, c]
        yy = lax.rem(y + 4 - back, 4)
        return a_o.at[:, lax.rem(yy, 2), c, :, pl.ds(pl.multiple_of(lax.div(yy, 2) * 512, 512), 512)]

    def half(p, ref, i):
        return ref.at[pl.ds(48 * i, 48)] if p == "q" else ref.at[pl.ds(2 * i, 2)]

    def along(p, k):
        return dev(dz=k) if p == "q" else dev(dy=k)

    def push(p, sid, src, dst, slot, to):
        row = sid if p == "q" else 2
        cp = remote(src, dst, s2s.at[row, slot], s2r.at[row, slot], to)
        cp.start()
        pending.append(cp)

    def arrived(p, sid, ref, slot):
        drain(ref, s2r.at[sid if p == "q" else 2, slot])

    def stream(p, sid, src):
        mine = piece(p, sid, 0)
        push(p, sid, src, mine, 0, along(p, 1))
        push(p, sid, src, mine, 1, along(p, 3))
        push(p, sid, src, mine, 4, sib)

    def second(p):
        cps, here = stage[p]
        for cp in cps:
            cp.wait_recv()
        here.wait()
        pending.extend(cps)
        sid = 1 if p == "q" else 0
        stream(p, sid, piece(p, sid, 0))

    def forward(p, sid, k):
        part = piece(p, sid, k)
        if k == 2:
            arrived(p, sid, half(p, part, 0), 2)
            arrived(p, sid, half(p, part, 1), 3)
        else:
            i = k // 2
            arrived(p, sid, part, i)
            push(p, sid, half(p, part, i), half(p, part, i), 2 + i, along(p, k))
        push(p, sid, part, part, 4 + k, sib)

    ready = set()

    def rows_ready(p):
        if p not in ready:
            ready.add(p)
            for sid in range(2 if p == "q" else 1):
                for k in range(4):
                    arrived(p, sid, piece(p, sid, 0), 4 + k)

    def weights_q(ch):
        @pl.loop(0, 8)
        def _(d):
            for half in range(2):
                block = lax.div(d, 2) * 4 + half * 2 + lax.rem(d, 2)
                col = pl.multiple_of(block * 1152 + ch * 128, 128)
                s = sc_q[0, block * 9 + ch]
                snd_q[ch, d, :, half * 128:(half + 1) * 128] = (
                    in_q[:, pl.ds(col, 128)].astype(F32) * s).astype(BF16)
        here = pl.ds(pl.multiple_of((z * 2 + c) * 128, 128), 128)
        for k, dc in ((2, 0), (2, 1), (1, 0), (3, 0), (1, 1), (3, 1), (0, 1)):
            slot = lax.rem(z + k, 4) * 2 + lax.rem(c + dc, 2)
            remote(snd_q.at[ch, slot], w_q.at[ch, here], wsq.at[ch], wrq.at[ch], dev(dz=k, dc=dc)).start()
        pltpu.make_async_copy(snd_q.at[ch, z * 2 + c], w_q.at[ch, here], wrq.at[ch]).start()

    def weights_o(ch):
        @pl.loop(0, 8)
        def _(d):
            for zz in range(4):
                block = zz * 4 + lax.rem(d, 4)
                tile = block * 8 + lax.div(d, 4) * 4 + ch
                col = pl.multiple_of(tile * 128, 128)
                s = sc_o[0, tile]
                snd_o[ch, d, :, zz * 128:(zz + 1) * 128] = (
                    in_o[:, pl.ds(col, 128)].astype(F32) * s).astype(BF16)
        here = pl.ds(pl.multiple_of((y * 2 + c) * 128, 128), 128)
        for k, dc in ((2, 0), (2, 1), (1, 0), (3, 0), (1, 1), (3, 1), (0, 1)):
            slot = lax.rem(y + k, 4) * 2 + lax.rem(c + dc, 2)
            remote(snd_o.at[ch, slot], w_o.at[ch, here], wso.at[ch], wro.at[ch], dev(dy=k, dc=dc)).start()
        pltpu.make_async_copy(snd_o.at[ch, y * 2 + c], w_o.at[ch, here], wro.at[ch]).start()

    loaded = set()

    def weights(p, ch):
        if p not in loaded:
            loaded.add(p)
            i = "qo".index(p)
            drain((in_q, in_o)[i], ld.at[2 + i])
            loads[-2 + i].wait()
        (weights_q if p == "q" else weights_o)(ch)

    class Chunk:
        def __init__(self, p, ch):
            swapped = (p, ch) in SWAPPED
            at = PLACE[p, ch]
            self.p, self.ch, self.swapped = p, ch, swapped
            self.part = p_q if p == "q" else p_o
            if p == "q":
                self.far, self.rx = (far_qs, rx_qs) if swapped else (far_q, rx_q)
                self.far_sems, self.rx_sems = (fsq, frq), (rsq, rrq)
            else:
                self.far, self.rx = (far_os, rx_os) if swapped else (far_o, rx_o)
                self.far_sems, self.rx_sems = (fso, fro), (rso, rro)
            self.far, self.rx = self.far.at[at], self.rx.at[at]
            if not swapped:
                self.me, self.right, self.left = x, dev(dx=1), dev(dx=3)
            elif p == "q":
                self.me, self.right, self.left = y, dev(dy=1), dev(dy=3)
            else:
                self.me, self.right, self.left = z, dev(dz=1), dev(dz=3)

        def block(self, ahead, half):
            to = lax.rem(self.me + ahead, 4)
            if not self.swapped:
                return self.part.at[self.ch, half, to]
            if self.p == "q":
                cols = pl.ds(pl.multiple_of(lax.rem(to, 2) * 128, 128), 128)
                return self.part.at[self.ch, lax.div(to, 2), pl.ds(2 * half, 2), :, cols]
            cols = pl.ds(pl.multiple_of(to * 128, 128), 128)
            return self.part.at[self.ch, half, :, :, cols]

        def send_far(self, src, half, to):
            ss, rs = self.far_sems
            remote(src, self.far.at[half], ss.at[self.ch, half], rs.at[self.ch, half], to).start()

        def send_sum(self, src, slot, to):
            ss, rs = self.rx_sems
            remote(src, self.rx.at[slot], ss.at[self.ch, slot], rs.at[self.ch, slot], to).start()

    def compute(p, ch):
        t = Chunk(p, ch)
        a, wt, wr, wide = (a_q, w_q, wrq, QW) if p == "q" else (a_o, w_o, wro, OW)
        rows_ready(p)
        drain(wt.at[ch], wr.at[ch])

        @pl.loop(0, 4)
        def _(i):
            lhs = a[i].reshape(384, 1024)
            acc = jnp.dot(lhs, wt[ch], preferred_element_type=F32)
            t.part[ch, lax.div(i, 2), pl.ds(lax.rem(i, 2) * 2, 2)] = acc.astype(BF16).reshape(2, 192, wide)

        t.send_far(t.block(2, 1), 1, t.right)
        t.send_far(t.block(2, 0), 0, t.left)
        t.send_sum(t.block(1, 0), 0, t.right)
        t.send_sum(t.block(3, 1), 1, t.left)

    def relay(p, ch):
        t = Chunk(p, ch)
        for half, ahead, slot, to in ((1, 1, 2, t.right), (0, 3, 3, t.left)):
            drain(t.far.at[half], t.far_sems[1].at[ch, half])
            own = t.block(ahead, half)
            own[...] = (own[...].astype(F32) + t.far[half].astype(F32)).astype(BF16)
            t.send_sum(own, slot, to)

    def collect(p, ch):
        t = Chunk(p, ch)
        for half, (i, j) in enumerate(((0, 3), (1, 2))):
            drain(t.rx.at[i], t.rx_sems[1].at[ch, i])
            drain(t.rx.at[j], t.rx_sems[1].at[ch, j])
            own = t.block(0, half)
            own[...] = (own[...].astype(F32) + t.rx[i].astype(F32) + t.rx[j].astype(F32)).astype(BF16)
        for k in (2, 1, 3):
            xx, yy, zz = lax.rem(x + k, 4), lax.rem(y + k, 4), lax.rem(z + k, 4)
            if p == "q":
                hh, ll = (yh, yl) if t.swapped else (lax.div(yy, 2), lax.rem(yy, 2))
                src = p_q.at[ch, hh, xx if t.swapped else x, :, pl.ds(pl.multiple_of(ll * 128, 128), 128)]
                to = dev(dx=k) if t.swapped else dev(dy=k)
                remote(src, ph_q.at[ch, k - 1], psq.at[ch, k - 1], prq.at[ch, k - 1], to).start()
            else:
                cols = pl.ds(pl.multiple_of((z if t.swapped else zz) * 128, 128), 128)
                src = p_o.at[ch, :, xx if t.swapped else x, :, cols]
                to = dev(dx=k) if t.swapped else dev(dz=k)
                remote(src, ph_o.at[ch, k - 1], pso.at[ch, k - 1], pro.at[ch, k - 1], to).start()

    def finish(p, ch):
        if p == "q":
            cols = pl.ds(pl.multiple_of(yl * 128, 128), 128)
            total = p_q[ch, yh, x, :, cols].astype(F32)
            for k in range(3):
                drain(ph_q.at[ch, k], prq.at[ch, k])
                total += ph_q[ch, k].astype(F32)
            out_q[:, ch * 128:(ch + 1) * 128] = total.astype(BF16)
        else:
            cols = pl.ds(pl.multiple_of(z * 128, 128), 128)
            for k in range(3):
                drain(ph_o.at[ch, k], pro.at[ch, k])
            give, keep = 1 - yh, yh
            for h in (give, keep):
                total = p_o[ch, h, x, :, cols].astype(F32)
                for k in range(3):
                    total += ph_o[ch, k, h].astype(F32)
                if h is give:
                    swap[0, ch] = total.astype(BF16)
                    remote(swap.at[0, ch], swap.at[1, ch], sws.at[ch], swr.at[ch], dev(dy=2)).start()
                else:
                    out_o[:, pl.ds(pl.multiple_of(yh * 512 + ch * 128, 128), 128)] = total.astype(BF16)

    def settle(ch):
        drain(swap.at[1, ch], swr.at[ch])
        out_o[:, pl.ds(pl.multiple_of((1 - yh) * 512 + ch * 128, 128), 128)] = swap[1, ch]

    todo = {
        "q1": first_q, "o1": first_o, "q2": lambda: second("q"), "o2": lambda: second("o"),
        "F": forward, "w": weights, "c": compute, "r": relay, "k": collect, "f": finish,
    }
    for op in OPS:
        todo[op[0]](*op[1:])
    for ch in range(OCH):
        settle(ch)

    for cp in pending:
        cp.wait_send()
    for ch in range(QCH):
        drain(snd_q.at[ch, pl.ds(0, 7)], wsq.at[ch])
    for ch in range(OCH):
        drain(snd_o.at[ch, pl.ds(0, 7)], wso.at[ch])
        drain(swap.at[0, ch], sws.at[ch])
    for p, ch in CHUNKS:
        t = Chunk(p, ch)
        for i in range(2):
            drain(t.far.at[i], t.far_sems[0].at[ch, i])
        for i in range(4):
            drain(t.rx.at[i], t.rx_sems[0].at[ch, i])
        ph, ps = (ph_q, psq) if p == "q" else (ph_o, pso)
        for k in range(3):
            drain(ph.at[ch, k], ps.at[ch, k])


def place_kernel(a, b, out_a, out_b):
    out_a[...] = a[...]
    out_b[...] = b[...]


def local(decode_rows, attended, qkv_values, qkv_scales, out_values, out_scales):
    dma = pltpu.SemaphoreType.DMA
    vmem = pltpu.VMEM
    sums = pl.pallas_call(
        kernel,
        out_shape=(
            jax.ShapeDtypeStruct((192, 1152), BF16),
            jax.ShapeDtypeStruct((192, 1024), BF16),
        ),
        in_specs=[pl.BlockSpec(memory_space=pl.ANY)] * 4 + [pl.BlockSpec(memory_space=vmem)] * 2,
        out_specs=(pl.BlockSpec(memory_space=vmem), pl.BlockSpec(memory_space=vmem)),
        scratch_shapes=[
            vmem((128, 18432), BF16), vmem((128, 16384), BF16),
            vmem((2, 96, 1024), BF16), vmem((4, 96, 512), BF16),
            vmem((4, 2, 2, 96, 1024), BF16), vmem((4, 2, 2, 96, 1024), BF16),
            vmem((QCH, 8, 128, QW), BF16), vmem((OCH, 8, 128, OW), BF16),
            vmem((QCH, 1024, QW), BF16), vmem((OCH, 1024, OW), BF16),
            vmem((QCH, 2, 4, 192, QW), BF16), vmem((OCH, 2, 4, 192, OW), BF16),
            vmem((QCH - NQS, 2, 192, QW), BF16), vmem((OCH - NOS, 2, 192, OW), BF16),
            vmem((NQS, 2, 2, 192, 128), BF16), vmem((NOS, 2, 4, 192, 128), BF16),
            vmem((QCH - NQS, 4, 192, QW), BF16), vmem((OCH - NOS, 4, 192, OW), BF16),
            vmem((NQS, 4, 2, 192, 128), BF16), vmem((NOS, 4, 4, 192, 128), BF16),
            vmem((QCH, 3, 192, 128), BF16), vmem((OCH, 3, 2, 192, 128), BF16),
            vmem((2, OCH, 192, 128), BF16),
            vmem((1, 144), F32), vmem((1, 128), F32), pltpu.SMEM((1, 144), F32), pltpu.SMEM((1, 128), F32),
            dma((6,)), dma((4,)), dma((2,)), dma((4,)), dma((3, 8)), dma((3, 8)),
            dma((QCH,)), dma((OCH,)), dma((QCH,)), dma((OCH,)),
            dma((QCH, 2)), dma((OCH, 2)), dma((QCH, 2)), dma((OCH, 2)),
            dma((QCH, 4)), dma((OCH, 4)), dma((QCH, 4)), dma((OCH, 4)),
            dma((QCH, 3)), dma((OCH, 3)), dma((QCH, 3)), dma((OCH, 3)),
            dma((OCH,)), dma((OCH,)),
        ],
        compiler_params=pltpu.CompilerParams(
            collective_id=0, has_side_effects=True, vmem_limit_bytes=63 * 2**20
        ),
        cost_estimate=pl.CostEstimate(flops=13_690_000_000, bytes_accessed=20_000_000, transcendentals=0),
        name="project",
    )(
        decode_rows, attended, qkv_values, out_values,
        qkv_scales, out_scales,
    )
    return pl.pallas_call(
        place_kernel,
        out_shape=tuple(jax.ShapeDtypeStruct(s.shape, BF16) for s in sums),
        in_specs=[pl.BlockSpec(memory_space=vmem)] * 2,
        out_specs=tuple([pl.BlockSpec(memory_space=vmem)] * 2),
        compiler_params=pltpu.CompilerParams(vmem_limit_bytes=4 * 2**20),
        name="place",
    )(*sums)


def solution(mesh):
    in_specs = (
        P("yz", "gx"),
        P("yz", "gx"),
        P(("gx", "yz"), None),
        P(("gx", "yz"), None),
        P(("gx", "yz"), None),
        P(("gx", "yz"), None),
    )
    out_specs = (P("gx", "yz"), P("gx", "yz"))
    return jax.shard_map(local, mesh=mesh, in_specs=in_specs, out_specs=out_specs, check_vma=False)
```

```python
import jax
import jax.numpy as jnp
from jax import lax
from jax.experimental import pallas as pl
from jax.experimental.pallas import tpu as pltpu
from jax.sharding import PartitionSpec as P

MESH = pl.DeviceIdType.MESH
F32 = jnp.float32
BF16 = jnp.bfloat16

QCH, QW = 9, 256
OCH, OW = 4, 512
SWAPPED = (("o", 2, 0), ("o", 2, 1), ("o", 3, 0), ("q", 0), ("q", 1), ("q", 2), ("q", 4), ("q", 5),)
RELAYED = (("o", 0, 0), ("o", 1, 0), ("o", 1, 1), ("o", 2, 0), ("o", 2, 1), ("o", 3, 0), ("q", 0), ("q", 1), ("q", 2), ("q", 3), ("q", 6), ("q", 7), ("q", 8),)
CHUNKS = tuple(("q", i) for i in range(QCH)) + tuple(("o", i) for i in range(OCH))
UNITS = tuple(("q", i) for i in range(QCH)) + tuple(("o", i, e) for i in range(OCH) for e in range(2))
PLACE = {}
for _p in "qo":
    for _kind in (False, True):
        for _i, _t in enumerate(t for t in UNITS if t[0] == _p and (t in SWAPPED) == _kind):
            PLACE[_t] = _i
NQS, NOS = (sum(t[0] == p for t in SWAPPED) for p in "qo")
OPS = (
    ("q1",), ("w", "o", 1), ("o1",), ("q2",), ("F", "q", 0, 1), ("F", "q", 0, 3), ("w", "q", 7), ("o2",),
    ("F", "q", 1, 1), ("F", "q", 1, 3), ("F", "q", 0, 2), ("w", "o", 2), ("w", "q", 3), ("w", "q", 1),
    ("F", "q", 1, 2), ("F", "o", 0, 1), ("F", "o", 0, 3), ("c", "q", 7), ("w", "q", 6), ("w", "q", 2),
    ("w", "o", 0), ("w", "q", 0), ("w", "o", 3), ("w", "q", 4), ("w", "q", 8), ("w", "q", 5), ("c", "q", 3),
    ("r", "q", 7), ("c", "q", 1), ("r", "q", 3), ("F", "o", 0, 2), ("c", "q", 6), ("k", "q", 7),
    ("c", "o", 1), ("k", "q", 3), ("c", "o", 2), ("c", "q", 2), ("r", "q", 6), ("c", "o", 0), ("c", "q", 0),
    ("r", "o", 1, 1), ("r", "o", 1, 0), ("c", "q", 4), ("k", "q", 6), ("c", "o", 3), ("c", "q", 8),
    ("r", "q", 1), ("r", "o", 0, 1), ("s", "q", 7), ("r", "o", 0, 0), ("s", "q", 3), ("r", "q", 2),
    ("k", "o", 1, 1), ("c", "q", 5), ("k", "o", 1, 0), ("r", "o", 2, 1), ("r", "q", 0), ("r", "o", 3, 1),
    ("r", "o", 2, 0), ("r", "q", 4), ("r", "q", 8), ("s", "q", 6), ("r", "o", 3, 0), ("k", "o", 0, 1),
    ("k", "q", 1), ("s", "o", 1, 1), ("f", "q", 7), ("f", "q", 3), ("k", "o", 0, 0), ("s", "o", 1, 0),
    ("k", "q", 2), ("k", "o", 3, 1), ("k", "o", 2, 1), ("r", "q", 5), ("k", "q", 8), ("s", "q", 1),
    ("k", "o", 2, 0), ("s", "q", 2), ("s", "o", 2, 1), ("k", "o", 3, 0), ("f", "q", 1), ("k", "q", 0),
    ("s", "o", 2, 0), ("f", "o", 0, 1), ("f", "q", 2), ("f", "o", 1, 1), ("k", "q", 4), ("f", "o", 2, 1),
    ("s", "o", 0, 0), ("s", "o", 3, 0), ("f", "q", 6), ("f", "o", 1, 0), ("s", "q", 0), ("k", "q", 5),
    ("f", "o", 2, 0), ("s", "q", 8), ("f", "o", 3, 1), ("f", "o", 0, 0), ("f", "q", 4), ("f", "o", 3, 0),
    ("f", "q", 0), ("f", "q", 8), ("f", "q", 5),
)


def kernel(
    rows_q, rows_o, val_q, val_o, scale_q, scale_o,
    out_q, out_o,
    in_q, in_o, x_q, x_o, a_q, a_o, snd_q, snd_o, w_q, w_o, p_q, p_o,
    far_q, far_o, far_qs, far_os, rx_q, rx_o, rx_qs, rx_os, ph_q, ph_o, swap, o_q, o_o, scf_q, scf_o, sc_q, sc_o,
    ld, s1s, s1q, s1o, s2s, s2r,
    wsq, wso, wrq, wro, fsq, fso, frq, fro, rsq, rso, rrq, rro, psq, pso, prq, pro, sws, swr, outs,
):
    g = lax.axis_index("gx")
    w = lax.axis_index("yz")
    x, yh = lax.rem(g, 4), lax.div(g, 4)
    c, yl, z = lax.rem(w, 2), lax.rem(lax.div(w, 2), 2), lax.div(w, 4)
    y = yh * 2 + yl

    def dev(dx=0, dy=0, dz=0, dc=0):
        xx, yy, zz, cc = (lax.rem(x + dx, 4), lax.rem(y + dy, 4), lax.rem(z + dz, 4), lax.rem(c + dc, 2))
        return (lax.div(yy, 2) * 4 + xx, zz * 4 + lax.rem(yy, 2) * 2 + cc)

    mate = (g, z * 4 + (1 - yl) * 2 + c)
    sib = dev(dc=1)

    def remote(src, dst, ssem, rsem, to):
        return pltpu.make_async_remote_copy(
            src_ref=src, dst_ref=dst, send_sem=ssem, recv_sem=rsem, device_id=to, device_id_type=MESH
        )

    def drain(ref, sem):
        pltpu.make_async_copy(ref, ref, sem).wait()

    loads = []
    for half in range(2):
        for zz in range(4):
            loads.append(pltpu.make_async_copy(
                rows_q.at[:, pl.ds(zz * 512 + half * 256, 256)],
                x_q.at[half, :, pl.ds(zz * 256, 256)], ld.at[0]))
    for zz in range(4):
        loads.append(pltpu.make_async_copy(
            rows_o.at[:, pl.ds(zz * 512, 512)], x_o.at[zz], ld.at[1]))
    loads.append(pltpu.make_async_copy(val_q, in_q, ld.at[2]))
    loads.append(pltpu.make_async_copy(val_o, in_o, ld.at[3]))
    for cp in loads:
        cp.start()

    scf_q[...] = scale_q[...].astype(F32)
    scf_o[...] = scale_o[...].astype(F32)
    for src, dst, sem in ((scf_q, sc_q, ld.at[4]), (scf_o, sc_o, ld.at[5])):
        cp = pltpu.make_async_copy(src, dst, sem)
        cp.start()
        loads.append(cp)

    peers = [dev(dy=dy, dz=dz) for dy in range(4) for dz in range(4) if (dy, dz) != (0, 0)]
    peers += [dev(dz=dz, dc=1) for dz in range(4)]
    peers += [dev(dy=dy, dc=1) for dy in range(1, 4)]
    peers += [dev(dx=1), dev(dx=2), dev(dx=3)]
    barrier = pltpu.get_barrier_semaphore()
    for peer in peers:
        pl.semaphore_signal(barrier, inc=1, device_id=peer, device_id_type=MESH)
    pl.semaphore_wait(barrier, len(peers))

    own_cols = pl.ds(pl.multiple_of(yh * 512, 512), 512)
    pending = []
    stage = {}

    def first_q():
        drain(x_q, ld.at[0])
        cp = remote(x_q.at[1 - yl], a_q.at[z, yl, c], s1s.at[0], s1q.at[0], mate)
        cp.start()
        here = pltpu.make_async_copy(x_q.at[yl], a_q.at[z, yl, c], s1q.at[1])
        here.start()
        stage["q"] = [cp], here
        stream("q", 0, x_q.at[yl])

    def first_o():
        drain(x_o, ld.at[1])
        cps = []
        for k in (2, 1, 3):
            cp = remote(x_o.at[lax.rem(z + k, 4)], a_o.at[z, yl, c, :, own_cols], s1s.at[k], s1o.at[k], dev(dz=k))
            cp.start()
            cps.append(cp)
        here = pltpu.make_async_copy(x_o.at[z], a_o.at[z, yl, c, :, own_cols], s1o.at[0])
        here.start()
        stage["o"] = cps, here

    def piece(p, sid, back):
        if p == "q":
            return a_q.at[lax.rem(z + 4 - back, 4), yl if sid == 0 else 1 - yl, c]
        yy = lax.rem(y + 4 - back, 4)
        return a_o.at[:, lax.rem(yy, 2), c, :, pl.ds(pl.multiple_of(lax.div(yy, 2) * 512, 512), 512)]

    def half(p, ref, i):
        return ref.at[pl.ds(48 * i, 48)] if p == "q" else ref.at[pl.ds(2 * i, 2)]

    def along(p, k):
        return dev(dz=k) if p == "q" else dev(dy=k)

    def push(p, sid, src, dst, slot, to):
        row = sid if p == "q" else 2
        cp = remote(src, dst, s2s.at[row, slot], s2r.at[row, slot], to)
        cp.start()
        pending.append(cp)

    def arrived(p, sid, ref, slot):
        drain(ref, s2r.at[sid if p == "q" else 2, slot])

    def stream(p, sid, src):
        mine = piece(p, sid, 0)
        push(p, sid, src, mine, 0, along(p, 1))
        push(p, sid, src, mine, 1, along(p, 3))
        push(p, sid, src, mine, 4, sib)

    def second(p):
        cps, here = stage[p]
        for cp in cps:
            cp.wait_recv()
        here.wait()
        pending.extend(cps)
        sid = 1 if p == "q" else 0
        stream(p, sid, piece(p, sid, 0))

    def forward(p, sid, k):
        part = piece(p, sid, k)
        if k == 2:
            arrived(p, sid, half(p, part, 0), 2)
            arrived(p, sid, half(p, part, 1), 3)
        else:
            i = k // 2
            arrived(p, sid, part, i)
            push(p, sid, half(p, part, i), half(p, part, i), 2 + i, along(p, k))
        push(p, sid, part, part, 4 + k, sib)

    ready = set()

    def rows_ready(p):
        if p not in ready:
            ready.add(p)
            if len(ready) == 2:
                for cp in pending:
                    cp.wait_send()
                pending.clear()
            for sid in range(2 if p == "q" else 1):
                for k in range(4):
                    arrived(p, sid, piece(p, sid, 0), 4 + k)

    def weights_q(ch):
        @pl.loop(0, 8)
        def _(d):
            for half in range(2):
                block = lax.div(d, 2) * 4 + half * 2 + lax.rem(d, 2)
                col = pl.multiple_of(block * 1152 + ch * 128, 128)
                s = sc_q[0, block * 9 + ch]
                snd_q[ch, d, :, half * 128:(half + 1) * 128] = (
                    in_q[:, pl.ds(col, 128)].astype(F32) * s).astype(BF16)
        here = pl.ds(pl.multiple_of((z * 2 + c) * 128, 128), 128)
        for k, dc in ((2, 0), (2, 1), (1, 0), (3, 0), (1, 1), (3, 1), (0, 1)):
            slot = lax.rem(z + k, 4) * 2 + lax.rem(c + dc, 2)
            remote(snd_q.at[ch, slot], w_q.at[ch, here], wsq.at[ch], wrq.at[ch], dev(dz=k, dc=dc)).start()
        pltpu.make_async_copy(snd_q.at[ch, z * 2 + c], w_q.at[ch, here], wrq.at[ch]).start()

    def weights_o(ch):
        @pl.loop(0, 8)
        def _(d):
            for zz in range(4):
                block = zz * 4 + lax.rem(d, 4)
                tile = block * 8 + lax.div(d, 4) * 4 + ch
                col = pl.multiple_of(tile * 128, 128)
                s = sc_o[0, tile]
                snd_o[ch, d, :, zz * 128:(zz + 1) * 128] = (
                    in_o[:, pl.ds(col, 128)].astype(F32) * s).astype(BF16)
        here = pl.ds(pl.multiple_of((y * 2 + c) * 128, 128), 128)
        for k, dc in ((2, 0), (2, 1), (1, 0), (3, 0), (1, 1), (3, 1), (0, 1)):
            slot = lax.rem(y + k, 4) * 2 + lax.rem(c + dc, 2)
            remote(snd_o.at[ch, slot], w_o.at[ch, here], wso.at[ch], wro.at[ch], dev(dy=k, dc=dc)).start()
        pltpu.make_async_copy(snd_o.at[ch, y * 2 + c], w_o.at[ch, here], wro.at[ch]).start()

    loaded = set()

    def weights(p, ch):
        if p not in loaded:
            loaded.add(p)
            i = "qo".index(p)
            drain((in_q, in_o)[i], ld.at[2 + i])
            loads[-2 + i].wait()
        (weights_q if p == "q" else weights_o)(ch)

    class Unit:
        def __init__(self, p, ch, e=None):
            key = (p, ch) if p == "q" else (p, ch, e)
            swapped = key in SWAPPED
            at = PLACE[key]
            self.p, self.ch, self.e, self.swapped, self.relayed = p, ch, e, swapped, key in RELAYED
            if p == "q":
                self.far, self.rx = (far_qs, rx_qs) if swapped else (far_q, rx_q)
                self.n, self.ph = ch, ph_q.at[ch]
                self.far_sems, self.rx_sems, self.ph_sems = (fsq, frq), (rsq, rrq), (psq, prq)
            else:
                self.far, self.rx = (far_os, rx_os) if swapped else (far_o, rx_o)
                self.n = 2 * ch + e
                self.ph = ph_o.at[self.n]
                self.rows = yh if e == 0 else 1 - yh
                self.far_sems, self.rx_sems, self.ph_sems = (fso, fro), (rso, rro), (pso, pro)
            self.far, self.rx = self.far.at[at], self.rx.at[at]
            if not swapped:
                self.me, self.right, self.left = x, dev(dx=1), dev(dx=3)
            elif p == "q":
                self.me, self.right, self.left = y, dev(dy=1), dev(dy=3)
            else:
                self.me, self.right, self.left = z, dev(dz=1), dev(dz=3)

        def block(self, ahead, half):
            to = lax.rem(self.me + ahead, 4)
            if self.p == "q":
                if not self.swapped:
                    return p_q.at[self.ch, half, to]
                cols = pl.ds(pl.multiple_of(lax.rem(to, 2) * 128, 128), 128)
                return p_q.at[self.ch, lax.div(to, 2), pl.ds(2 * half, 2), :, :, cols]
            if not self.swapped:
                return p_o.at[self.ch, self.rows, to, half]
            cols = pl.ds(pl.multiple_of(to * 128, 128), 128)
            return p_o.at[self.ch, self.rows, pl.ds(2 * half, 2), :, :, cols]

        def last(self, ahead, half=None):
            if self.swapped:
                xx, yy, zz = lax.rem(x + ahead, 4), y, z
            else:
                xx, yy, zz = x, lax.rem(y + ahead, 4), lax.rem(z + ahead, 4)
            i = slice(None) if half is None else half
            if self.p == "q":
                cols = pl.ds(pl.multiple_of(lax.rem(yy, 2) * 128, 128), 128)
                return p_q.at[self.ch, lax.div(yy, 2), xx, i, :, cols]
            return p_o.at[self.ch, self.rows, xx, i, :, pl.ds(pl.multiple_of(zz * 128, 128), 128)]

        def toward(self, k):
            return dev(dx=k) if self.swapped else dev(dy=k) if self.p == "q" else dev(dz=k)

        def send(self, sems, src, dst, slot, to):
            remote(src, dst, sems[0].at[self.n, slot], sems[1].at[self.n, slot], to).start()

        def send_far(self, src, slot, to):
            self.send(self.far_sems, src, self.far.at[slot], slot, to)

        def send_sum(self, src, slot, to):
            self.send(self.rx_sems, src, self.rx.at[slot], slot, to)

        def send_last(self, src, slot, sem, to):
            self.send(self.ph_sems, src, self.ph.at[slot], sem, to)

        def far_done(self, slot, way):
            drain(self.far.at[slot], self.far_sems[way].at[self.n, slot])

        def sum_done(self, slot, way):
            drain(self.rx.at[slot], self.rx_sems[way].at[self.n, slot])

        def last_done(self, slot, sem, way):
            drain(self.ph.at[slot], self.ph_sems[way].at[self.n, sem])

    SENT, CAME = 0, 1

    def compute(p, ch):
        a, wt, wr, part, wide = (a_q, w_q, wrq, p_q, QW) if p == "q" else (a_o, w_o, wro, p_o, OW)
        rows_ready(p)
        drain(wt.at[ch], wr.at[ch])

        @pl.loop(0, 4)
        def _(i):
            lhs = a[i].reshape(384, 1024)
            acc = jnp.dot(lhs, wt[ch], preferred_element_type=F32)
            part[ch, lax.div(i, 2), pl.ds(lax.rem(i, 2) * 2, 2)] = acc.astype(BF16).reshape(2, 2, 96, wide)

        for t in (Unit(p, ch),) if p == "q" else (Unit(p, ch, 1), Unit(p, ch, 0)):
            t.send_far(t.block(2, 1), 1, t.right)
            t.send_far(t.block(2, 0), 0, t.left)
            t.send_sum(t.block(1, 0), 0, t.right)
            t.send_sum(t.block(3, 1), 1, t.left)
        snd, ws = (snd_q, wsq) if p == "q" else (snd_o, wso)
        drain(snd.at[ch, pl.ds(0, 7)], ws.at[ch])

    def relay(*unit):
        t = Unit(*unit)
        for half, ahead, slot, to in ((1, 1, 2, t.right), (0, 3, 3, t.left)):
            t.far_done(half, CAME)
            own = t.block(ahead, half)
            own[...] = (own[...].astype(F32) + t.far[half].astype(F32)).astype(BF16)
            t.send_sum(own, slot, to)

    def collect(*unit):
        t = Unit(*unit)
        for half, (i, j) in enumerate(((0, 3), (1, 2))):
            t.sum_done(i, CAME)
            t.sum_done(j, CAME)
            own = t.block(0, half)
            own[...] = (own[...].astype(F32) + t.rx[i].astype(F32) + t.rx[j].astype(F32)).astype(BF16)
        if t.relayed:
            t.send_last(t.last(2, 1), 1, 1, t.toward(1))
            t.send_last(t.last(2, 0), 0, 0, t.toward(3))
            t.send_last(t.last(1, 0), 2, 2, t.toward(1))
            t.send_last(t.last(3, 1), 3, 3, t.toward(3))
        else:
            for k in (2, 1, 3):
                t.send_last(t.last(k), pl.ds(2 * (k - 1), 2), k - 1, t.toward(k))
        for slot in range(2):
            t.far_done(slot, SENT)

    def relay_last(*unit):
        t = Unit(*unit)
        for half, ahead, slot in ((1, 1, 4), (0, 3, 5)):
            t.last_done(half, half, CAME)
            own = t.last(ahead, half)
            own[...] = (own[...].astype(F32) + t.ph[half].astype(F32)).astype(BF16)
            t.send_last(own, slot, slot, t.toward(ahead))

    placed = []

    def put(src, dst, i):
        cp = pltpu.make_async_copy(src, dst, outs.at[i])
        cp.start()
        placed.append(cp)

    def finish(*unit):
        t = Unit(*unit)
        p, ch = t.p, t.ch
        if t.relayed:
            terms = ((2, 5), (3, 4))
            for slot in range(2, 6):
                t.last_done(slot, slot, CAME)
        else:
            terms = ((0, 2, 4), (1, 3, 5))
            for k in range(3):
                t.last_done(pl.ds(2 * k, 2), k, CAME)
        if p == "q":
            to = o_q.at[ch]
        else:
            to = o_o.at[ch] if t.e == 0 else swap.at[0, ch]
        for i in range(2):
            v = t.last(0, i)[...].astype(F32)
            for slot in terms[i]:
                v += t.ph[slot].astype(F32)
            to[96 * i:96 * (i + 1)] = v.astype(BF16)
        if p == "q":
            put(to, out_q.at[:, ch * 128:(ch + 1) * 128], ch)
        elif t.e == 0:
            put(to, out_o.at[:, pl.ds(pl.multiple_of(yh * 512 + ch * 128, 128), 128)], QCH + ch)
        else:
            remote(swap.at[0, ch], swap.at[1, ch], sws.at[ch], swr.at[ch], dev(dy=2)).start()
        for slot in range(4):
            t.sum_done(slot, SENT)

    def settle(ch):
        drain(swap.at[1, ch], swr.at[ch])
        put(swap.at[1, ch], out_o.at[:, pl.ds(pl.multiple_of((1 - yh) * 512 + ch * 128, 128), 128)], QCH + OCH + ch)

    todo = {
        "q1": first_q, "o1": first_o, "q2": lambda: second("q"), "o2": lambda: second("o"),
        "F": forward, "w": weights, "c": compute, "r": relay, "k": collect,
        "s": relay_last, "f": finish,
    }
    for op in OPS:
        todo[op[0]](*op[1:])
    for ch in range(OCH):
        settle(ch)

    for cp in pending:
        cp.wait_send()
    for ch in range(OCH):
        drain(swap.at[0, ch], sws.at[ch])
    for unit in UNITS:
        t = Unit(*unit)
        if t.relayed:
            for slot in range(6):
                t.last_done(slot, slot, SENT)
        else:
            for k in range(3):
                t.last_done(pl.ds(2 * k, 2), k, SENT)
    for cp in placed:
        cp.wait()


def place_kernel(a, b, out_a, out_b):
    out_a[...] = a[...]
    out_b[...] = b[...]


def local(decode_rows, attended, qkv_values, qkv_scales, out_values, out_scales):
    dma = pltpu.SemaphoreType.DMA
    vmem = pltpu.VMEM
    sums = pl.pallas_call(
        kernel,
        out_shape=(
            jax.ShapeDtypeStruct((192, 1152), BF16),
            jax.ShapeDtypeStruct((192, 1024), BF16),
        ),
        in_specs=[pl.BlockSpec(memory_space=pl.ANY)] * 4 + [pl.BlockSpec(memory_space=vmem)] * 2,
        out_specs=(pl.BlockSpec(memory_space=pl.ANY), pl.BlockSpec(memory_space=pl.ANY)),
        scratch_shapes=[
            vmem((128, 18432), BF16), vmem((128, 16384), BF16),
            vmem((2, 96, 1024), BF16), vmem((4, 96, 512), BF16),
            vmem((4, 2, 2, 96, 1024), BF16), vmem((4, 2, 2, 96, 1024), BF16),
            vmem((QCH, 8, 128, QW), BF16), vmem((OCH, 8, 128, OW), BF16),
            vmem((QCH, 1024, QW), BF16), vmem((OCH, 1024, OW), BF16),
            vmem((QCH, 2, 4, 2, 96, QW), BF16), vmem((OCH, 2, 4, 2, 96, OW), BF16),
            vmem((QCH - NQS, 2, 2, 96, QW), BF16), vmem((2 * OCH - NOS, 2, 96, OW), BF16),
            vmem((NQS, 2, 2, 2, 96, 128), BF16), vmem((NOS, 2, 2, 2, 96, 128), BF16),
            vmem((QCH - NQS, 4, 2, 96, QW), BF16), vmem((2 * OCH - NOS, 4, 96, OW), BF16),
            vmem((NQS, 4, 2, 2, 96, 128), BF16), vmem((NOS, 4, 2, 2, 96, 128), BF16),
            vmem((QCH, 6, 96, 128), BF16), vmem((2 * OCH, 6, 96, 128), BF16),
            vmem((2, OCH, 192, 128), BF16), vmem((QCH, 192, 128), BF16), vmem((OCH, 192, 128), BF16),
            vmem((1, 144), F32), vmem((1, 128), F32), pltpu.SMEM((1, 144), F32), pltpu.SMEM((1, 128), F32),
            dma((6,)), dma((4,)), dma((2,)), dma((4,)), dma((3, 8)), dma((3, 8)),
            dma((QCH,)), dma((OCH,)), dma((QCH,)), dma((OCH,)),
            dma((QCH, 2)), dma((2 * OCH, 2)), dma((QCH, 2)), dma((2 * OCH, 2)),
            dma((QCH, 4)), dma((2 * OCH, 4)), dma((QCH, 4)), dma((2 * OCH, 4)),
            dma((QCH, 6)), dma((2 * OCH, 6)), dma((QCH, 6)), dma((2 * OCH, 6)),
            dma((OCH,)), dma((OCH,)), dma((QCH + 2 * OCH,)),
        ],
        compiler_params=pltpu.CompilerParams(
            collective_id=0, has_side_effects=True, vmem_limit_bytes=63 * 2**20
        ),
        cost_estimate=pl.CostEstimate(flops=13_690_000_000, bytes_accessed=20_000_000, transcendentals=0),
        name="project",
    )(
        decode_rows, attended, qkv_values, out_values,
        qkv_scales, out_scales,
    )
    return pl.pallas_call(
        place_kernel,
        out_shape=tuple(jax.ShapeDtypeStruct(s.shape, BF16) for s in sums),
        in_specs=[pl.BlockSpec(memory_space=vmem)] * 2,
        out_specs=tuple([pl.BlockSpec(memory_space=vmem)] * 2),
        compiler_params=pltpu.CompilerParams(vmem_limit_bytes=63 * 2**20),
        name="place",
    )(*sums)


def solution(mesh):
    in_specs = (
        P("yz", "gx"),
        P("yz", "gx"),
        P(("gx", "yz"), None),
        P(("gx", "yz"), None),
        P(("gx", "yz"), None),
        P(("gx", "yz"), None),
    )
    out_specs = (P("gx", "yz"), P("gx", "yz"))
    return jax.shard_map(local, mesh=mesh, in_specs=in_specs, out_specs=out_specs, check_vma=False)
```

```python
import jax
import jax.numpy as jnp
from jax import lax
from jax.experimental import pallas as pl
from jax.experimental.pallas import tpu as pltpu
from jax.sharding import PartitionSpec as P

MESH = pl.DeviceIdType.MESH
F32 = jnp.float32
BF16 = jnp.bfloat16

QCH, QW = 9, 256
OCH, OW = 4, 512
SWAPPED = (("o", 2, 0), ("o", 2, 1), ("o", 3, 0), ("q", 0), ("q", 1), ("q", 2), ("q", 4), ("q", 5),)
RELAYED = (("o", 0, 0), ("o", 1, 0), ("o", 1, 1), ("o", 2, 0), ("o", 2, 1), ("o", 3, 0), ("q", 0), ("q", 1), ("q", 2), ("q", 3), ("q", 6), ("q", 7), ("q", 8),)
CHUNKS = tuple(("q", i) for i in range(QCH)) + tuple(("o", i) for i in range(OCH))
UNITS = tuple(("q", i) for i in range(QCH)) + tuple(("o", i, e) for i in range(OCH) for e in range(2))
PLACE = {}
for _p in "qo":
    for _kind in (False, True):
        for _i, _t in enumerate(t for t in UNITS if t[0] == _p and (t in SWAPPED) == _kind):
            PLACE[_t] = _i
NQS, NOS = (sum(t[0] == p for t in SWAPPED) for p in "qo")
OPS = (
    ("q1",), ("w", "o", 1), ("o1",), ("q2",), ("F", "q", 0, 1), ("F", "q", 0, 3), ("w", "q", 7), ("o2",),
    ("F", "q", 1, 1), ("F", "q", 1, 3), ("F", "q", 0, 2), ("w", "o", 2), ("w", "q", 3), ("w", "q", 1),
    ("F", "q", 1, 2), ("F", "o", 0, 1), ("F", "o", 0, 3), ("c", "q", 7), ("w", "q", 6), ("w", "q", 2),
    ("w", "o", 0), ("w", "q", 0), ("w", "o", 3), ("w", "q", 4), ("w", "q", 8), ("w", "q", 5), ("c", "q", 3),
    ("r", "q", 7), ("c", "q", 1), ("r", "q", 3), ("F", "o", 0, 2), ("c", "q", 6), ("k", "q", 7),
    ("c", "o", 1), ("k", "q", 3), ("c", "o", 2), ("c", "q", 2), ("r", "q", 6), ("c", "o", 0), ("c", "q", 0),
    ("r", "o", 1, 1), ("r", "o", 1, 0), ("c", "q", 4), ("k", "q", 6), ("c", "o", 3), ("c", "q", 8),
    ("r", "q", 1), ("r", "o", 0, 1), ("s", "q", 7), ("r", "o", 0, 0), ("s", "q", 3), ("r", "q", 2),
    ("k", "o", 1, 1), ("c", "q", 5), ("k", "o", 1, 0), ("r", "o", 2, 1), ("r", "q", 0), ("r", "o", 3, 1),
    ("r", "o", 2, 0), ("r", "q", 4), ("r", "q", 8), ("s", "q", 6), ("r", "o", 3, 0), ("k", "o", 0, 1),
    ("k", "q", 1), ("s", "o", 1, 1), ("f", "q", 7), ("f", "q", 3), ("k", "o", 0, 0), ("s", "o", 1, 0),
    ("k", "q", 2), ("k", "o", 3, 1), ("k", "o", 2, 1), ("r", "q", 5), ("k", "q", 8), ("s", "q", 1),
    ("k", "o", 2, 0), ("s", "q", 2), ("s", "o", 2, 1), ("k", "o", 3, 0), ("f", "q", 1), ("k", "q", 0),
    ("s", "o", 2, 0), ("f", "o", 0, 1), ("f", "q", 2), ("f", "o", 1, 1), ("k", "q", 4), ("f", "o", 2, 1),
    ("s", "o", 0, 0), ("s", "o", 3, 0), ("f", "q", 6), ("f", "o", 1, 0), ("s", "q", 0), ("k", "q", 5),
    ("f", "o", 2, 0), ("s", "q", 8), ("f", "o", 3, 1), ("f", "o", 0, 0), ("f", "q", 4), ("f", "o", 3, 0),
    ("f", "q", 0), ("f", "q", 8), ("f", "q", 5),
)


def kernel(
    rows_q, rows_o, val_q, val_o, scale_q, scale_o,
    out_q, out_o,
    in_q, in_o, x_q, x_o, a_q, a_o, snd_q, snd_o, w_q, w_o, p_q, p_o,
    far_q, far_o, far_qs, far_os, rx_q, rx_o, rx_qs, rx_os, ph_q, ph_o, swap, o_q, o_o, scb_q, scb_o, scf_q, scf_o, sc_q, sc_o,
    ld, s1s, s1r, s2s, s2r,
    ws, wrq, wro, ss, fr, rr, pr, sw, outs,
):
    g = lax.axis_index("gx")
    w = lax.axis_index("yz")
    x, yh = lax.rem(g, 4), lax.div(g, 4)
    c, yl, z = lax.rem(w, 2), lax.rem(lax.div(w, 2), 2), lax.div(w, 4)
    y = yh * 2 + yl

    def dev(dx=0, dy=0, dz=0, dc=0):
        xx, yy, zz, cc = (lax.rem(x + dx, 4), lax.rem(y + dy, 4), lax.rem(z + dz, 4), lax.rem(c + dc, 2))
        return (lax.div(yy, 2) * 4 + xx, zz * 4 + lax.rem(yy, 2) * 2 + cc)

    mate = (g, z * 4 + (1 - yl) * 2 + c)
    sib = dev(dc=1)

    def remote(src, dst, ssem, rsem, to):
        return pltpu.make_async_remote_copy(
            src_ref=src, dst_ref=dst, send_sem=ssem, recv_sem=rsem, device_id=to, device_id_type=MESH
        )

    def drain(ref, sem):
        pltpu.make_async_copy(ref, ref, sem).wait()

    loads = []
    for half in range(2):
        for zz in range(4):
            loads.append(pltpu.make_async_copy(
                rows_q.at[:, pl.ds(zz * 512 + half * 256, 256)],
                x_q.at[half, :, pl.ds(zz * 256, 256)], ld.at[0]))
    for zz in range(4):
        loads.append(pltpu.make_async_copy(
            rows_o.at[:, pl.ds(zz * 512, 512)], x_o.at[zz], ld.at[1]))
    scales = [pltpu.make_async_copy(scale_q, scb_q, ld.at[4]), pltpu.make_async_copy(scale_o, scb_o, ld.at[5])]
    loads += scales
    loads.append(pltpu.make_async_copy(val_q, in_q, ld.at[2]))
    loads.append(pltpu.make_async_copy(val_o, in_o, ld.at[3]))
    for cp in loads:
        cp.start()

    peers = [dev(dy=dy, dz=dz) for dy in range(4) for dz in range(4) if (dy, dz) != (0, 0)]
    peers += [dev(dz=dz, dc=1) for dz in range(4)]
    peers += [dev(dy=dy, dc=1) for dy in range(1, 4)]
    peers += [dev(dx=1), dev(dx=2), dev(dx=3)]
    barrier = pltpu.get_barrier_semaphore()
    for peer in peers:
        pl.semaphore_signal(barrier, inc=1, device_id=peer, device_id_type=MESH)
    pl.semaphore_wait(barrier, len(peers))

    own_cols = pl.ds(pl.multiple_of(yh * 512, 512), 512)

    def first_q():
        drain(x_q, ld.at[0])
        cp = remote(x_q.at[1 - yl], a_q.at[z, yl, c], s1s.at[0], s1r.at[0], mate)
        cp.start()
        pltpu.make_async_copy(x_q.at[yl], a_q.at[z, yl, c], s1r.at[0]).start()
        stream("q", 0, x_q.at[yl])

    def first_o():
        drain(x_o, ld.at[1])
        for k in (2, 1, 3):
            remote(x_o.at[lax.rem(z + k, 4)], a_o.at[z, yl, c, :, own_cols], s1s.at[1], s1r.at[1], dev(dz=k)).start()
        pltpu.make_async_copy(x_o.at[z], a_o.at[z, yl, c, :, own_cols], s1r.at[1]).start()

    def piece(p, sid, back):
        if p == "q":
            return a_q.at[lax.rem(z + 4 - back, 4), yl if sid == 0 else 1 - yl, c]
        yy = lax.rem(y + 4 - back, 4)
        return a_o.at[:, lax.rem(yy, 2), c, :, pl.ds(pl.multiple_of(lax.div(yy, 2) * 512, 512), 512)]

    def half(p, ref, i):
        return ref.at[pl.ds(48 * i, 48)] if p == "q" else ref.at[pl.ds(2 * i, 2)]

    def along(p, k):
        return dev(dz=k) if p == "q" else dev(dy=k)

    def push(p, sid, src, dst, slot, to):
        row = sid if p == "q" else 2
        remote(src, dst, s2s.at[row], s2r.at[row, slot], to).start()

    def arrived(p, sid, ref, slot):
        drain(ref, s2r.at[sid if p == "q" else 2, slot])

    def stream(p, sid, src):
        mine = piece(p, sid, 0)
        push(p, sid, src, mine, 0, along(p, 1))
        push(p, sid, src, mine, 1, along(p, 3))
        push(p, sid, src, mine, 3, sib)

    def second(p):
        drain(x_q if p == "q" else x_o, s1r.at["qo".index(p)])
        sid = 1 if p == "q" else 0
        stream(p, sid, piece(p, sid, 0))

    def forward(p, sid, k):
        part = piece(p, sid, k)
        if k == 2:
            arrived(p, sid, part, 2)
        else:
            i = k // 2
            arrived(p, sid, part, i)
            push(p, sid, half(p, part, i), half(p, part, i), 2, along(p, k))
        push(p, sid, part, part, 3, sib)

    ready = set()

    def rows_ready(p):
        if p not in ready:
            ready.add(p)
            for sid in range(2 if p == "q" else 1):
                arrived(p, sid, a_q.at[:, 0, 0] if p == "q" else a_o.at[:, 0], 3)

    def weights_q(ch):
        @pl.loop(0, 8)
        def _(d):
            for half in range(2):
                block = lax.div(d, 2) * 4 + half * 2 + lax.rem(d, 2)
                col = pl.multiple_of(block * 1152 + ch * 128, 128)
                s = sc_q[0, block * 9 + ch]
                snd_q[ch, d, :, half * 128:(half + 1) * 128] = (
                    in_q[:, pl.ds(col, 128)].astype(F32) * s).astype(BF16)
        here = pl.ds(pl.multiple_of((z * 2 + c) * 128, 128), 128)
        for k, dc in ((2, 0), (2, 1), (1, 0), (3, 0), (1, 1), (3, 1), (0, 1)):
            slot = lax.rem(z + k, 4) * 2 + lax.rem(c + dc, 2)
            remote(snd_q.at[ch, slot], w_q.at[ch, here], ws.at[0], wrq.at[ch], dev(dz=k, dc=dc)).start()
        pltpu.make_async_copy(snd_q.at[ch, z * 2 + c], w_q.at[ch, here], wrq.at[ch]).start()

    def weights_o(ch):
        @pl.loop(0, 8)
        def _(d):
            for zz in range(4):
                block = zz * 4 + lax.rem(d, 4)
                tile = block * 8 + lax.div(d, 4) * 4 + ch
                col = pl.multiple_of(tile * 128, 128)
                s = sc_o[0, tile]
                snd_o[ch, d, :, zz * 128:(zz + 1) * 128] = (
                    in_o[:, pl.ds(col, 128)].astype(F32) * s).astype(BF16)
        here = pl.ds(pl.multiple_of((y * 2 + c) * 128, 128), 128)
        for k, dc in ((2, 0), (2, 1), (1, 0), (3, 0), (1, 1), (3, 1), (0, 1)):
            slot = lax.rem(y + k, 4) * 2 + lax.rem(c + dc, 2)
            remote(snd_o.at[ch, slot], w_o.at[ch, here], ws.at[1], wro.at[ch], dev(dy=k, dc=dc)).start()
        pltpu.make_async_copy(snd_o.at[ch, y * 2 + c], w_o.at[ch, here], wro.at[ch]).start()

    loaded = set()

    def weights(p, ch):
        if p not in loaded:
            loaded.add(p)
            i = "qo".index(p)
            scales[i].wait()
            wide, smem = ((scf_q, sc_q), (scf_o, sc_o))[i]
            wide[...] = (scb_q, scb_o)[i][...].astype(F32)
            cp = pltpu.make_async_copy(wide, smem, ld.at[4 + i])
            cp.start()
            cp.wait()
            drain((in_q, in_o)[i], ld.at[2 + i])
        (weights_q if p == "q" else weights_o)(ch)

    class Unit:
        def __init__(self, p, ch, e=None):
            key = (p, ch) if p == "q" else (p, ch, e)
            swapped = key in SWAPPED
            at = PLACE[key]
            self.p, self.ch, self.e, self.swapped, self.relayed = p, ch, e, swapped, key in RELAYED
            if p == "q":
                self.far, self.rx = (far_qs, rx_qs) if swapped else (far_q, rx_q)
                self.n, self.ph = ch, ph_q.at[ch]
                self.sems = fr.at[self.n], rr.at[self.n], pr.at[self.n]
                self.sent = ss.at[1 if swapped else 0], ss.at[5 if swapped else 4], ss.at[8]
            else:
                self.far, self.rx = (far_os, rx_os) if swapped else (far_o, rx_o)
                self.n = 2 * ch + e
                self.ph = ph_o.at[self.n]
                self.rows = yh if e == 0 else 1 - yh
                self.sems = fr.at[QCH + self.n], rr.at[QCH + self.n], pr.at[QCH + self.n]
                self.sent = ss.at[3 if swapped else 2], ss.at[7 if swapped else 6], ss.at[9]
            self.far, self.rx = self.far.at[at], self.rx.at[at]
            if not swapped:
                self.me, self.right, self.left = x, dev(dx=1), dev(dx=3)
            elif p == "q":
                self.me, self.right, self.left = y, dev(dy=1), dev(dy=3)
            else:
                self.me, self.right, self.left = z, dev(dz=1), dev(dz=3)

        def block(self, ahead, half):
            to = lax.rem(self.me + ahead, 4)
            if self.p == "q":
                if not self.swapped:
                    return p_q.at[self.ch, half, to]
                cols = pl.ds(pl.multiple_of(lax.rem(to, 2) * 128, 128), 128)
                return p_q.at[self.ch, lax.div(to, 2), pl.ds(2 * half, 2), :, :, cols]
            if not self.swapped:
                return p_o.at[self.ch, self.rows, to, half]
            cols = pl.ds(pl.multiple_of(to * 128, 128), 128)
            return p_o.at[self.ch, self.rows, pl.ds(2 * half, 2), :, :, cols]

        def last(self, ahead, half=None):
            if self.swapped:
                xx, yy, zz = lax.rem(x + ahead, 4), y, z
            else:
                xx, yy, zz = x, lax.rem(y + ahead, 4), lax.rem(z + ahead, 4)
            i = slice(None) if half is None else half
            if self.p == "q":
                cols = pl.ds(pl.multiple_of(lax.rem(yy, 2) * 128, 128), 128)
                return p_q.at[self.ch, lax.div(yy, 2), xx, i, :, cols]
            return p_o.at[self.ch, self.rows, xx, i, :, pl.ds(pl.multiple_of(zz * 128, 128), 128)]

        def toward(self, k):
            return dev(dx=k) if self.swapped else dev(dy=k) if self.p == "q" else dev(dz=k)

        def send_far(self, src, slot, to):
            remote(src, self.far.at[slot], self.sent[0], self.sems[0], to).start()

        def send_sum(self, src, slot, to):
            remote(src, self.rx.at[slot], self.sent[1], self.sems[1], to).start()

        def send_last(self, src, slot, stage, to):
            remote(src, self.ph.at[slot], self.sent[2], self.sems[2].at[stage], to).start()

    def compute(p, ch):
        a, wt, wr, part, wide = (a_q, w_q, wrq, p_q, QW) if p == "q" else (a_o, w_o, wro, p_o, OW)
        rows_ready(p)
        drain(wt.at[ch], wr.at[ch])

        @pl.loop(0, 4)
        def _(i):
            lhs = a[i].reshape(384, 1024)
            acc = jnp.dot(lhs, wt[ch], preferred_element_type=F32)
            part[ch, lax.div(i, 2), pl.ds(lax.rem(i, 2) * 2, 2)] = acc.astype(BF16).reshape(2, 2, 96, wide)

        for t in (Unit(p, ch),) if p == "q" else (Unit(p, ch, 1), Unit(p, ch, 0)):
            t.send_far(t.block(2, 1), 1, t.right)
            t.send_far(t.block(2, 0), 0, t.left)
            t.send_sum(t.block(1, 0), 0, t.right)
            t.send_sum(t.block(3, 1), 1, t.left)

    def relay(*unit):
        t = Unit(*unit)
        drain(t.far, t.sems[0])
        for half, ahead, slot, to in ((1, 1, 2, t.right), (0, 3, 3, t.left)):
            own = t.block(ahead, half)
            own[...] = (own[...].astype(F32) + t.far[half].astype(F32)).astype(BF16)
            t.send_sum(own, slot, to)

    def collect(*unit):
        t = Unit(*unit)
        drain(t.rx, t.sems[1])
        for half, (i, j) in enumerate(((0, 3), (1, 2))):
            own = t.block(0, half)
            own[...] = (own[...].astype(F32) + t.rx[i].astype(F32) + t.rx[j].astype(F32)).astype(BF16)
        if t.relayed:
            t.send_last(t.last(2, 1), 1, 0, t.toward(1))
            t.send_last(t.last(2, 0), 0, 0, t.toward(3))
            t.send_last(t.last(1, 0), 2, 1, t.toward(1))
            t.send_last(t.last(3, 1), 3, 1, t.toward(3))
        else:
            for k in (2, 1, 3):
                t.send_last(t.last(k), pl.ds(2 * (k - 1), 2), 1, t.toward(k))

    def relay_last(*unit):
        t = Unit(*unit)
        drain(t.ph.at[pl.ds(0, 2)], t.sems[2].at[0])
        for half, ahead, slot in ((1, 1, 4), (0, 3, 5)):
            own = t.last(ahead, half)
            own[...] = (own[...].astype(F32) + t.ph[half].astype(F32)).astype(BF16)
            t.send_last(own, slot, 1, t.toward(ahead))

    def put(src, dst, i):
        pltpu.make_async_copy(src, dst, outs.at[i]).start()

    def finish(*unit):
        t = Unit(*unit)
        p, ch = t.p, t.ch
        if t.relayed:
            terms = ((2, 5), (3, 4))
            drain(t.ph.at[pl.ds(2, 4)], t.sems[2].at[1])
        else:
            terms = ((0, 2, 4), (1, 3, 5))
            drain(t.ph, t.sems[2].at[1])
        if p == "q":
            to = o_q.at[ch]
        else:
            to = o_o.at[ch] if t.e == 0 else swap.at[0, ch]
        for i in range(2):
            v = t.last(0, i)[...].astype(F32)
            for slot in terms[i]:
                v += t.ph[slot].astype(F32)
            to[96 * i:96 * (i + 1)] = v.astype(BF16)
        if p == "q":
            put(to, out_q.at[:, ch * 128:(ch + 1) * 128], 0)
        elif t.e == 0:
            put(to, out_o.at[:, pl.ds(pl.multiple_of(yh * 512 + ch * 128, 128), 128)], 1)
        else:
            remote(swap.at[0, ch], swap.at[1, ch], sw.at[0], sw.at[1], dev(dy=2)).start()

    todo = {
        "q1": first_q, "o1": first_o, "q2": lambda: second("q"), "o2": lambda: second("o"),
        "F": forward, "w": weights, "c": compute, "r": relay, "k": collect,
        "s": relay_last, "f": finish,
    }
    for op in OPS:
        todo[op[0]](*op[1:])
    drain(swap.at[1], sw.at[1])
    for ch in range(OCH):
        put(swap.at[1, ch], out_o.at[:, pl.ds(pl.multiple_of((1 - yh) * 512 + ch * 128, 128), 128)], 2)

    drain(x_q.at[0], s1s.at[0])
    drain(x_o.at[pl.ds(0, 3)], s1s.at[1])
    for row, n in ((0, 3), (1, 3), (2, 6)):
        drain(snd_q.at[pl.ds(0, n), pl.ds(0, 7)], s2s.at[row])
    drain(snd_q.at[:, pl.ds(0, 7)], ws.at[0])
    drain(snd_o.at[:, pl.ds(0, 7)], ws.at[1])
    for i, ref in enumerate((far_q, far_qs, far_o, far_os, rx_q, rx_qs, rx_o, rx_os, ph_q, ph_o)):
        drain(ref, ss.at[i])
    drain(swap.at[0], sw.at[0])
    for i, ref in enumerate((o_q, o_o, swap.at[1])):
        drain(ref, outs.at[i])


def place_kernel(a, b, out_a, out_b, va, vb, sems):
    ins, outs = [], []
    for i, (src, mid, dst) in enumerate(((a, va, out_a), (b, vb, out_b))):
        for j in range(4):
            rows = pl.ds(48 * j, 48)
            ins.append(pltpu.make_async_copy(src.at[rows], mid.at[rows], sems.at[0, 4 * i + j]))
            outs.append(pltpu.make_async_copy(mid.at[rows], dst.at[rows], sems.at[1, 4 * i + j]))
    for cp in ins:
        cp.start()
    for cp, after in zip(ins, outs):
        cp.wait()
        after.start()
    for cp in outs:
        cp.wait()


def local(decode_rows, attended, qkv_values, qkv_scales, out_values, out_scales):
    dma = pltpu.SemaphoreType.DMA
    vmem = pltpu.VMEM
    sums = pl.pallas_call(
        kernel,
        out_shape=(
            jax.ShapeDtypeStruct((192, 1152), BF16),
            jax.ShapeDtypeStruct((192, 1024), BF16),
        ),
        in_specs=[pl.BlockSpec(memory_space=pl.ANY)] * 6,
        out_specs=(pl.BlockSpec(memory_space=pl.ANY), pl.BlockSpec(memory_space=pl.ANY)),
        scratch_shapes=[
            vmem((128, 18432), BF16), vmem((128, 16384), BF16),
            vmem((2, 96, 1024), BF16), vmem((4, 96, 512), BF16),
            vmem((4, 2, 2, 96, 1024), BF16), vmem((4, 2, 2, 96, 1024), BF16),
            vmem((QCH, 8, 128, QW), BF16), vmem((OCH, 8, 128, OW), BF16),
            vmem((QCH, 1024, QW), BF16), vmem((OCH, 1024, OW), BF16),
            vmem((QCH, 2, 4, 2, 96, QW), BF16), vmem((OCH, 2, 4, 2, 96, OW), BF16),
            vmem((QCH - NQS, 2, 2, 96, QW), BF16), vmem((2 * OCH - NOS, 2, 96, OW), BF16),
            vmem((NQS, 2, 2, 2, 96, 128), BF16), vmem((NOS, 2, 2, 2, 96, 128), BF16),
            vmem((QCH - NQS, 4, 2, 96, QW), BF16), vmem((2 * OCH - NOS, 4, 96, OW), BF16),
            vmem((NQS, 4, 2, 2, 96, 128), BF16), vmem((NOS, 4, 2, 2, 96, 128), BF16),
            vmem((QCH, 6, 96, 128), BF16), vmem((2 * OCH, 6, 96, 128), BF16),
            vmem((2, OCH, 192, 128), BF16), vmem((QCH, 192, 128), BF16), vmem((OCH, 192, 128), BF16),
            vmem((1, 144), BF16), vmem((1, 128), BF16), vmem((1, 144), F32), vmem((1, 128), F32), pltpu.SMEM((1, 144), F32), pltpu.SMEM((1, 128), F32),
            dma((6,)), dma((2,)), dma((2,)), dma((3,)), dma((3, 4)),
            dma((2,)), dma((QCH,)), dma((OCH,)), dma((10,)),
            dma((len(UNITS),)), dma((len(UNITS),)), dma((len(UNITS), 2)), dma((2,)), dma((3,)),
        ],
        compiler_params=pltpu.CompilerParams(
            collective_id=0, has_side_effects=True, vmem_limit_bytes=63 * 2**20
        ),
        cost_estimate=pl.CostEstimate(flops=13_690_000_000, bytes_accessed=20_000_000, transcendentals=0),
        name="project",
    )(
        decode_rows, attended, qkv_values, out_values,
        qkv_scales, out_scales,
    )
    return pl.pallas_call(
        place_kernel,
        out_shape=tuple(jax.ShapeDtypeStruct(s.shape, BF16) for s in sums),
        in_specs=[pl.BlockSpec(memory_space=pl.ANY)] * 2,
        out_specs=tuple([pl.BlockSpec(memory_space=pl.ANY)] * 2),
        scratch_shapes=[vmem((192, 1152), BF16), vmem((192, 1024), BF16), dma((2, 8))],
        compiler_params=pltpu.CompilerParams(vmem_limit_bytes=63 * 2**20),
        name="place",
    )(*sums)


def solution(mesh):
    in_specs = (
        P("yz", "gx"),
        P("yz", "gx"),
        P(("gx", "yz"), None),
        P(("gx", "yz"), None),
        P(("gx", "yz"), None),
        P(("gx", "yz"), None),
    )
    out_specs = (P("gx", "yz"), P("gx", "yz"))
    return jax.shard_map(local, mesh=mesh, in_specs=in_specs, out_specs=out_specs, check_vma=False)
```

```python
import jax
import jax.numpy as jnp
from jax import lax
from jax.experimental import pallas as pl
from jax.experimental.pallas import tpu as pltpu
from jax.sharding import PartitionSpec as P

MESH = pl.DeviceIdType.MESH
F32 = jnp.float32
BF16 = jnp.bfloat16

QCH, QW = 9, 256
OCH, OW = 4, 512
SWAPPED = (("o", 2, 0), ("o", 2, 1), ("o", 3, 0), ("q", 0), ("q", 1), ("q", 2), ("q", 4), ("q", 5),)
RELAYED = (("o", 0, 0), ("o", 1, 0), ("o", 1, 1), ("o", 2, 0), ("o", 2, 1), ("o", 3, 0), ("q", 0), ("q", 1), ("q", 2), ("q", 3), ("q", 6), ("q", 7), ("q", 8),)
CHUNKS = tuple(("q", i) for i in range(QCH)) + tuple(("o", i) for i in range(OCH))
UNITS = tuple(("q", i) for i in range(QCH)) + tuple(("o", i, e) for i in range(OCH) for e in range(2))
PLACE = {}
for _p in "qo":
    for _kind in (False, True):
        for _i, _t in enumerate(t for t in UNITS if t[0] == _p and (t in SWAPPED) == _kind):
            PLACE[_t] = _i
NQS, NOS = (sum(t[0] == p for t in SWAPPED) for p in "qo")
OPS = (
    ("q1",), ("w", "o", 1), ("o1",), ("q2",), ("F", "q", 0, 1), ("F", "q", 0, 3), ("w", "q", 7), ("o2",),
    ("F", "q", 1, 1), ("F", "q", 1, 3), ("F", "q", 0, 2), ("w", "o", 2), ("w", "q", 3), ("w", "q", 1),
    ("F", "q", 1, 2), ("F", "o", 0, 1), ("F", "o", 0, 3), ("c", "q", 7), ("w", "q", 6), ("w", "q", 2),
    ("w", "o", 0), ("w", "q", 0), ("w", "o", 3), ("w", "q", 4), ("w", "q", 8), ("w", "q", 5), ("c", "q", 3),
    ("r", "q", 7), ("c", "q", 1), ("r", "q", 3), ("F", "o", 0, 2), ("c", "q", 6), ("k", "q", 7),
    ("c", "o", 1), ("k", "q", 3), ("c", "o", 2), ("c", "q", 2), ("r", "q", 6), ("c", "o", 0), ("c", "q", 0),
    ("r", "o", 1, 1), ("r", "o", 1, 0), ("c", "q", 4), ("k", "q", 6), ("c", "o", 3), ("c", "q", 8),
    ("r", "q", 1), ("r", "o", 0, 1), ("s", "q", 7), ("r", "o", 0, 0), ("s", "q", 3), ("r", "q", 2),
    ("k", "o", 1, 1), ("c", "q", 5), ("k", "o", 1, 0), ("r", "o", 2, 1), ("r", "q", 0), ("r", "o", 3, 1),
    ("r", "o", 2, 0), ("r", "q", 4), ("r", "q", 8), ("s", "q", 6), ("r", "o", 3, 0), ("k", "o", 0, 1),
    ("k", "q", 1), ("s", "o", 1, 1), ("f", "q", 7), ("f", "q", 3), ("k", "o", 0, 0), ("s", "o", 1, 0),
    ("k", "q", 2), ("k", "o", 3, 1), ("k", "o", 2, 1), ("r", "q", 5), ("k", "q", 8), ("s", "q", 1),
    ("k", "o", 2, 0), ("s", "q", 2), ("s", "o", 2, 1), ("k", "o", 3, 0), ("f", "q", 1), ("k", "q", 0),
    ("s", "o", 2, 0), ("f", "o", 0, 1), ("f", "q", 2), ("f", "o", 1, 1), ("k", "q", 4), ("f", "o", 2, 1),
    ("s", "o", 0, 0), ("s", "o", 3, 0), ("f", "q", 6), ("f", "o", 1, 0), ("s", "q", 0), ("k", "q", 5),
    ("f", "o", 2, 0), ("s", "q", 8), ("f", "o", 3, 1), ("f", "o", 0, 0), ("f", "q", 4), ("f", "o", 3, 0),
    ("f", "q", 0), ("f", "q", 8), ("f", "q", 5),
)


def kernel(
    rows_q, rows_o, val_q, val_o, scale_q, scale_o,
    out_q, out_o,
    in_q, in_o, x_q, x_o, a_q, a_o, snd_q, snd_o, w_q, w_o, p_q, p_o,
    far_q, far_o, far_qs, far_os, rx_q, rx_o, rx_qs, rx_os, ph_q, ph_o, swap, scb_q, scb_o, scf_q, scf_o, sc_q, sc_o,
    ld, s1s, s1r, s2s, s2r,
    ws, wrq, wro, ss, fr, rr, pr, sw,
):
    g = lax.axis_index("gx")
    w = lax.axis_index("yz")
    x, yh = lax.rem(g, 4), lax.div(g, 4)
    c, yl, z = lax.rem(w, 2), lax.rem(lax.div(w, 2), 2), lax.div(w, 4)
    y = yh * 2 + yl

    def dev(dx=0, dy=0, dz=0, dc=0):
        xx, yy, zz, cc = (lax.rem(x + dx, 4), lax.rem(y + dy, 4), lax.rem(z + dz, 4), lax.rem(c + dc, 2))
        return (lax.div(yy, 2) * 4 + xx, zz * 4 + lax.rem(yy, 2) * 2 + cc)

    mate = (g, z * 4 + (1 - yl) * 2 + c)
    sib = dev(dc=1)

    def remote(src, dst, ssem, rsem, to):
        return pltpu.make_async_remote_copy(
            src_ref=src, dst_ref=dst, send_sem=ssem, recv_sem=rsem, device_id=to, device_id_type=MESH
        )

    def drain(ref, sem):
        pltpu.make_async_copy(ref, ref, sem).wait()

    peers = [dev(dy=dy, dz=dz) for dy in range(4) for dz in range(4) if (dy, dz) != (0, 0)]
    peers += [dev(dz=dz, dc=1) for dz in range(4)]
    peers += [dev(dy=dy, dc=1) for dy in range(1, 4)]
    peers += [dev(dx=1), dev(dx=2), dev(dx=3)]
    barrier = pltpu.get_barrier_semaphore()
    for peer in peers:
        pl.semaphore_signal(barrier, inc=1, device_id=peer, device_id_type=MESH)

    loads = []
    for half in range(2):
        for zz in range(4):
            loads.append(pltpu.make_async_copy(
                rows_q.at[:, pl.ds(zz * 512 + half * 256, 256)],
                x_q.at[half, :, pl.ds(zz * 256, 256)], ld.at[0]))
    for zz in range(4):
        loads.append(pltpu.make_async_copy(
            rows_o.at[:, pl.ds(zz * 512, 512)], x_o.at[zz], ld.at[1]))
    scales = [pltpu.make_async_copy(scale_q, scb_q, ld.at[4]), pltpu.make_async_copy(scale_o, scb_o, ld.at[5])]
    loads += scales
    loads.append(pltpu.make_async_copy(val_q, in_q, ld.at[2]))
    loads.append(pltpu.make_async_copy(val_o, in_o, ld.at[3]))
    for cp in loads:
        cp.start()

    pl.semaphore_wait(barrier, len(peers))

    own_cols = pl.ds(pl.multiple_of(yh * 512, 512), 512)

    def first_q():
        drain(x_q, ld.at[0])
        cp = remote(x_q.at[1 - yl], a_q.at[z, yl, c], s1s.at[0], s1r.at[0], mate)
        cp.start()
        pltpu.make_async_copy(x_q.at[yl], a_q.at[z, yl, c], s1r.at[0]).start()
        stream("q", 0, x_q.at[yl])

    def first_o():
        drain(x_o, ld.at[1])
        for k in (2, 1, 3):
            remote(x_o.at[lax.rem(z + k, 4)], a_o.at[z, yl, c, :, own_cols], s1s.at[1], s1r.at[1], dev(dz=k)).start()
        pltpu.make_async_copy(x_o.at[z], a_o.at[z, yl, c, :, own_cols], s1r.at[1]).start()

    def piece(p, sid, back):
        if p == "q":
            return a_q.at[lax.rem(z + 4 - back, 4), yl if sid == 0 else 1 - yl, c]
        yy = lax.rem(y + 4 - back, 4)
        return a_o.at[:, lax.rem(yy, 2), c, :, pl.ds(pl.multiple_of(lax.div(yy, 2) * 512, 512), 512)]

    def half(p, ref, i):
        return ref.at[pl.ds(48 * i, 48)] if p == "q" else ref.at[pl.ds(2 * i, 2)]

    def along(p, k):
        return dev(dz=k) if p == "q" else dev(dy=k)

    def push(p, sid, src, dst, slot, to):
        row = sid if p == "q" else 2
        remote(src, dst, s2s.at[row], s2r.at[row, slot], to).start()

    def arrived(p, sid, ref, slot):
        drain(ref, s2r.at[sid if p == "q" else 2, slot])

    def stream(p, sid, src):
        mine = piece(p, sid, 0)
        push(p, sid, src, mine, 0, along(p, 1))
        push(p, sid, src, mine, 1, along(p, 3))
        push(p, sid, src, mine, 3, sib)

    def second(p):
        drain(x_q if p == "q" else x_o, s1r.at["qo".index(p)])
        sid = 1 if p == "q" else 0
        stream(p, sid, piece(p, sid, 0))

    def forward(p, sid, k):
        part = piece(p, sid, k)
        if k == 2:
            arrived(p, sid, part, 2)
        else:
            i = k // 2
            arrived(p, sid, part, i)
            push(p, sid, half(p, part, i), half(p, part, i), 2, along(p, k))
        push(p, sid, part, part, 3, sib)

    ready = set()

    def rows_ready(p):
        if p not in ready:
            ready.add(p)
            for sid in range(2 if p == "q" else 1):
                arrived(p, sid, a_q.at[:, 0, 0] if p == "q" else a_o.at[:, 0], 3)

    def weights_q(ch):
        @pl.loop(0, 8)
        def _(d):
            for half in range(2):
                block = lax.div(d, 2) * 4 + half * 2 + lax.rem(d, 2)
                col = pl.multiple_of(block * 1152 + ch * 128, 128)
                s = sc_q[0, block * 9 + ch]
                snd_q[ch, d, :, half * 128:(half + 1) * 128] = (
                    in_q[:, pl.ds(col, 128)].astype(F32) * s).astype(BF16)
        here = pl.ds(pl.multiple_of((z * 2 + c) * 128, 128), 128)
        for k, dc in ((2, 0), (2, 1), (1, 0), (3, 0), (1, 1), (3, 1), (0, 1)):
            slot = lax.rem(z + k, 4) * 2 + lax.rem(c + dc, 2)
            remote(snd_q.at[ch, slot], w_q.at[ch, here], ws.at[0], wrq.at[ch], dev(dz=k, dc=dc)).start()
        pltpu.make_async_copy(snd_q.at[ch, z * 2 + c], w_q.at[ch, here], wrq.at[ch]).start()

    def weights_o(ch):
        @pl.loop(0, 8)
        def _(d):
            for zz in range(4):
                block = zz * 4 + lax.rem(d, 4)
                tile = block * 8 + lax.div(d, 4) * 4 + ch
                col = pl.multiple_of(tile * 128, 128)
                s = sc_o[0, tile]
                snd_o[ch, d, :, zz * 128:(zz + 1) * 128] = (
                    in_o[:, pl.ds(col, 128)].astype(F32) * s).astype(BF16)
        here = pl.ds(pl.multiple_of((y * 2 + c) * 128, 128), 128)
        for k, dc in ((2, 0), (2, 1), (1, 0), (3, 0), (1, 1), (3, 1), (0, 1)):
            slot = lax.rem(y + k, 4) * 2 + lax.rem(c + dc, 2)
            remote(snd_o.at[ch, slot], w_o.at[ch, here], ws.at[1], wro.at[ch], dev(dy=k, dc=dc)).start()
        pltpu.make_async_copy(snd_o.at[ch, y * 2 + c], w_o.at[ch, here], wro.at[ch]).start()

    loaded = set()

    def weights(p, ch):
        if p not in loaded:
            loaded.add(p)
            i = "qo".index(p)
            scales[i].wait()
            wide, smem = ((scf_q, sc_q), (scf_o, sc_o))[i]
            wide[...] = (scb_q, scb_o)[i][...].astype(F32)
            cp = pltpu.make_async_copy(wide, smem, ld.at[4 + i])
            cp.start()
            cp.wait()
            drain((in_q, in_o)[i], ld.at[2 + i])
        (weights_q if p == "q" else weights_o)(ch)

    class Unit:
        def __init__(self, p, ch, e=None):
            key = (p, ch) if p == "q" else (p, ch, e)
            swapped = key in SWAPPED
            at = PLACE[key]
            self.p, self.ch, self.e, self.swapped, self.relayed = p, ch, e, swapped, key in RELAYED
            if p == "q":
                self.far, self.rx = (far_qs, rx_qs) if swapped else (far_q, rx_q)
                self.n, self.ph = ch, ph_q.at[ch]
                self.sems = fr.at[self.n], rr.at[self.n], pr.at[self.n]
                self.sent = ss.at[1 if swapped else 0], ss.at[5 if swapped else 4], ss.at[8]
            else:
                self.far, self.rx = (far_os, rx_os) if swapped else (far_o, rx_o)
                self.n = 2 * ch + e
                self.ph = ph_o.at[self.n]
                self.rows = yh if e == 0 else 1 - yh
                self.sems = fr.at[QCH + self.n], rr.at[QCH + self.n], pr.at[QCH + self.n]
                self.sent = ss.at[3 if swapped else 2], ss.at[7 if swapped else 6], ss.at[9]
            self.far, self.rx = self.far.at[at], self.rx.at[at]
            if not swapped:
                self.me, self.right, self.left = x, dev(dx=1), dev(dx=3)
            elif p == "q":
                self.me, self.right, self.left = y, dev(dy=1), dev(dy=3)
            else:
                self.me, self.right, self.left = z, dev(dz=1), dev(dz=3)

        def block(self, ahead, half):
            to = lax.rem(self.me + ahead, 4)
            if self.p == "q":
                if not self.swapped:
                    return p_q.at[self.ch, half, to]
                cols = pl.ds(pl.multiple_of(lax.rem(to, 2) * 128, 128), 128)
                return p_q.at[self.ch, lax.div(to, 2), pl.ds(2 * half, 2), :, :, cols]
            if not self.swapped:
                return p_o.at[self.ch, self.rows, to, half]
            cols = pl.ds(pl.multiple_of(to * 128, 128), 128)
            return p_o.at[self.ch, self.rows, pl.ds(2 * half, 2), :, :, cols]

        def last(self, ahead, half=None):
            if self.swapped:
                xx, yy, zz = lax.rem(x + ahead, 4), y, z
            else:
                xx, yy, zz = x, lax.rem(y + ahead, 4), lax.rem(z + ahead, 4)
            i = slice(None) if half is None else half
            if self.p == "q":
                cols = pl.ds(pl.multiple_of(lax.rem(yy, 2) * 128, 128), 128)
                return p_q.at[self.ch, lax.div(yy, 2), xx, i, :, cols]
            return p_o.at[self.ch, self.rows, xx, i, :, pl.ds(pl.multiple_of(zz * 128, 128), 128)]

        def toward(self, k):
            return dev(dx=k) if self.swapped else dev(dy=k) if self.p == "q" else dev(dz=k)

        def send_far(self, src, slot, to):
            remote(src, self.far.at[slot], self.sent[0], self.sems[0], to).start()

        def send_sum(self, src, slot, to):
            remote(src, self.rx.at[slot], self.sent[1], self.sems[1], to).start()

        def send_last(self, src, slot, stage, to):
            remote(src, self.ph.at[slot], self.sent[2], self.sems[2].at[stage], to).start()

    def compute(p, ch):
        a, wt, wr, part, wide = (a_q, w_q, wrq, p_q, QW) if p == "q" else (a_o, w_o, wro, p_o, OW)
        rows_ready(p)
        drain(wt.at[ch], wr.at[ch])

        @pl.loop(0, 4)
        def _(i):
            lhs = a[i].reshape(384, 1024)
            acc = jnp.dot(lhs, wt[ch], preferred_element_type=F32)
            part[ch, lax.div(i, 2), pl.ds(lax.rem(i, 2) * 2, 2)] = acc.astype(BF16).reshape(2, 2, 96, wide)

        for t in (Unit(p, ch),) if p == "q" else (Unit(p, ch, 1), Unit(p, ch, 0)):
            t.send_far(t.block(2, 1), 1, t.right)
            t.send_far(t.block(2, 0), 0, t.left)
            t.send_sum(t.block(1, 0), 0, t.right)
            t.send_sum(t.block(3, 1), 1, t.left)

    def relay(*unit):
        t = Unit(*unit)
        drain(t.far, t.sems[0])
        for half, ahead, slot, to in ((1, 1, 2, t.right), (0, 3, 3, t.left)):
            own = t.block(ahead, half)
            own[...] = (own[...].astype(F32) + t.far[half].astype(F32)).astype(BF16)
            t.send_sum(own, slot, to)

    def collect(*unit):
        t = Unit(*unit)
        drain(t.rx, t.sems[1])
        for half, (i, j) in enumerate(((0, 3), (1, 2))):
            own = t.block(0, half)
            own[...] = (own[...].astype(F32) + t.rx[i].astype(F32) + t.rx[j].astype(F32)).astype(BF16)
        if t.relayed:
            t.send_last(t.last(2, 1), 1, 0, t.toward(1))
            t.send_last(t.last(2, 0), 0, 0, t.toward(3))
            t.send_last(t.last(1, 0), 2, 1, t.toward(1))
            t.send_last(t.last(3, 1), 3, 1, t.toward(3))
        else:
            for k in (2, 1, 3):
                t.send_last(t.last(k), pl.ds(2 * (k - 1), 2), 1, t.toward(k))

    def relay_last(*unit):
        t = Unit(*unit)
        drain(t.ph.at[pl.ds(0, 2)], t.sems[2].at[0])
        for half, ahead, slot in ((1, 1, 4), (0, 3, 5)):
            own = t.last(ahead, half)
            own[...] = (own[...].astype(F32) + t.ph[half].astype(F32)).astype(BF16)
            t.send_last(own, slot, 1, t.toward(ahead))

    def finish(*unit):
        t = Unit(*unit)
        p, ch = t.p, t.ch
        if t.relayed:
            terms = ((2, 5), (3, 4))
            drain(t.ph.at[pl.ds(2, 4)], t.sems[2].at[1])
        else:
            terms = ((0, 2, 4), (1, 3, 5))
            drain(t.ph, t.sems[2].at[1])
        if p == "q":
            to = out_q.at[:, ch * 128:(ch + 1) * 128]
        elif t.e == 0:
            to = out_o.at[:, pl.ds(pl.multiple_of(yh * 512 + ch * 128, 128), 128)]
        else:
            to = swap.at[0, ch]
        for i in range(2):
            v = t.last(0, i)[...].astype(F32)
            for slot in terms[i]:
                v += t.ph[slot].astype(F32)
            to[96 * i:96 * (i + 1)] = v.astype(BF16)
        if p == "o" and t.e == 1:
            remote(swap.at[0, ch], swap.at[1, ch], sw.at[0], sw.at[1], dev(dy=2)).start()

    todo = {
        "q1": first_q, "o1": first_o, "q2": lambda: second("q"), "o2": lambda: second("o"),
        "F": forward, "w": weights, "c": compute, "r": relay, "k": collect,
        "s": relay_last, "f": finish,
    }
    for op in OPS:
        todo[op[0]](*op[1:])
    drain(swap.at[1], sw.at[1])
    for ch in range(OCH):
        out_o[:, pl.ds(pl.multiple_of((1 - yh) * 512 + ch * 128, 128), 128)] = swap[1, ch]

    drain(x_q.at[0], s1s.at[0])
    drain(x_o.at[pl.ds(0, 3)], s1s.at[1])
    for row, n in ((0, 3), (1, 3), (2, 6)):
        drain(snd_q.at[pl.ds(0, n), pl.ds(0, 7)], s2s.at[row])
    drain(snd_q.at[:, pl.ds(0, 7)], ws.at[0])
    drain(snd_o.at[:, pl.ds(0, 7)], ws.at[1])
    for i, ref in enumerate((far_q, far_qs, far_o, far_os, rx_q, rx_qs, rx_o, rx_os, ph_q, ph_o)):
        drain(ref, ss.at[i])
    drain(swap.at[0], sw.at[0])


def place_kernel(a, b, out_a, out_b):
    out_a[...] = a[...]
    out_b[...] = b[...]


def local(decode_rows, attended, qkv_values, qkv_scales, out_values, out_scales):
    dma = pltpu.SemaphoreType.DMA
    vmem = pltpu.VMEM
    sums = pl.pallas_call(
        kernel,
        out_shape=(
            vmem((192, 1152), BF16),
            vmem((192, 1024), BF16),
        ),
        in_specs=[pl.BlockSpec(memory_space=pl.ANY)] * 6,
        out_specs=(pl.BlockSpec(memory_space=vmem), pl.BlockSpec(memory_space=vmem)),
        scratch_shapes=[
            vmem((128, 18432), BF16), vmem((128, 16384), BF16),
            vmem((2, 96, 1024), BF16), vmem((4, 96, 512), BF16),
            vmem((4, 2, 2, 96, 1024), BF16), vmem((4, 2, 2, 96, 1024), BF16),
            vmem((QCH, 8, 128, QW), BF16), vmem((OCH, 8, 128, OW), BF16),
            vmem((QCH, 1024, QW), BF16), vmem((OCH, 1024, OW), BF16),
            vmem((QCH, 2, 4, 2, 96, QW), BF16), vmem((OCH, 2, 4, 2, 96, OW), BF16),
            vmem((QCH - NQS, 2, 2, 96, QW), BF16), vmem((2 * OCH - NOS, 2, 96, OW), BF16),
            vmem((NQS, 2, 2, 2, 96, 128), BF16), vmem((NOS, 2, 2, 2, 96, 128), BF16),
            vmem((QCH - NQS, 4, 2, 96, QW), BF16), vmem((2 * OCH - NOS, 4, 96, OW), BF16),
            vmem((NQS, 4, 2, 2, 96, 128), BF16), vmem((NOS, 4, 2, 2, 96, 128), BF16),
            vmem((QCH, 6, 96, 128), BF16), vmem((2 * OCH, 6, 96, 128), BF16),
            vmem((2, OCH, 192, 128), BF16),
            vmem((1, 144), BF16), vmem((1, 128), BF16), vmem((1, 144), F32), vmem((1, 128), F32), pltpu.SMEM((1, 144), F32), pltpu.SMEM((1, 128), F32),
            dma((6,)), dma((2,)), dma((2,)), dma((3,)), dma((3, 4)),
            dma((2,)), dma((QCH,)), dma((OCH,)), dma((10,)),
            dma((len(UNITS),)), dma((len(UNITS),)), dma((len(UNITS), 2)), dma((2,)),
        ],
        compiler_params=pltpu.CompilerParams(
            collective_id=0, has_side_effects=True, vmem_limit_bytes=61 * 2**20
        ),
        cost_estimate=pl.CostEstimate(flops=13_690_000_000, bytes_accessed=20_000_000, transcendentals=0),
        name="project",
    )(
        decode_rows, attended, qkv_values, out_values,
        qkv_scales, out_scales,
    )
    return pl.pallas_call(
        place_kernel,
        out_shape=tuple(jax.ShapeDtypeStruct(s.shape, BF16) for s in sums),
        in_specs=[pl.BlockSpec(memory_space=vmem)] * 2,
        out_specs=tuple([pl.BlockSpec(memory_space=vmem)] * 2),
        compiler_params=pltpu.CompilerParams(vmem_limit_bytes=4 * 2**20),
        name="place",
    )(*sums)


def solution(mesh):
    in_specs = (
        P("yz", "gx"),
        P("yz", "gx"),
        P(("gx", "yz"), None),
        P(("gx", "yz"), None),
        P(("gx", "yz"), None),
        P(("gx", "yz"), None),
    )
    out_specs = (P("gx", "yz"), P("gx", "yz"))
    return jax.shard_map(local, mesh=mesh, in_specs=in_specs, out_specs=out_specs, check_vma=False)
```
